32 devices in a mesh: dp: 16 (over z, x, core), mp: 2 (over y).
Axes of the slice: x: 2, y: 2, z: 4, core: 2. Of those that a mesh axis runs over, the one named last changes fastest.
Arguments:
- hidden_in: bfloat16 [8192, 768], P('dp'), may hold values from -6 to 6
- norm1_gain: float32 [768], replicated, may hold values from 0.5 to 1.5
- w_query: bfloat16 [768, 768], P(None, 'mp'), may hold values from -0.3125 to 0.3125
- w_key: bfloat16 [768, 768], P(None, 'mp'), may hold values from -0.21875 to 0.21875
- w_value: bfloat16 [768, 768], P(None, 'mp'), may hold values from -0.21875 to 0.21875
- w_output: bfloat16 [768, 768], P('mp'), may hold values from -1.25 to 1.25
- bias_table: float32 [32, 12], P(None, 'mp'), may hold values from -4 to 4
- bucket_ids: int32 [512, 512], replicated, may hold values from 0 to 31, as said below
- norm2_gain: float32 [768], replicated, may hold values from 0.5 to 1.5
- router: float32 [768, 16], replicated, may hold values from -0.109375 to 0.109375
- w_in: bfloat16 [16, 768, 3072], P('dp', None, 'mp'), may hold values from -0.21875 to 0.21875
- w_out: bfloat16 [16, 3072, 768], P('dp', 'mp'), may hold values from -1.75 to 1.75
- expert_ids: int32 [8192], P('dp'), may hold values from 0 to 15, as said below
- slot_ids: int32 [8192], P('dp'), may hold values from 0 to 39, as said below
- out_grad: bfloat16 [8192, 768], P('dp'), may hold values from -6 to 6
Outputs:
- hidden_out: bfloat16 [8192, 768], P('dp')
- grad_hidden_in: float32 [8192, 768], P('dp')
- grad_norm1_gain: float32 [768], replicated
- grad_w_query: float32 [768, 768], P(None, 'mp')
- grad_w_key: float32 [768, 768], P(None, 'mp')
- grad_w_value: float32 [768, 768], P(None, 'mp')
- grad_w_output: float32 [768, 768], P('mp')
- grad_bias_table: float32 [32, 12], P(None, 'mp')
- grad_norm2_gain: float32 [768], replicated
- grad_router: float32 [768, 16], replicated
- grad_w_in: float32 [16, 768, 3072], P('dp', None, 'mp')
- grad_w_out: float32 [16, 3072, 768], P('dp', 'mp')
The draws below stay inside these ranges and needn't reach their ends.
Inputs may be any that keep to these rules, and one draw needn't show every extreme that they name: `expert_ids`: among the 512 tokens of one device, no expert is named by more than 40 tokens and some expert by exactly 40; one expert is named by exactly 40 tokens of every device; every expert is named somewhere. `slot_ids`: tokens of one device that name the same expert have distinct slots. bucket_ids[i, j] depends only on j - i; keys at or before the query take the lower half of the buckets and later keys the upper half, and within each half the bucket does not fall as the distance grows.
All inputs are finite; a program needn't handle non-finite values.
Results may differ from the reference program's by a relative error of at most 0.018.
Values may be sent and summed in bfloat16 or wider, within the bound.
No kernel may reach another device: no remote copies, remote signals or barrier semaphores. Data moves between devices by JAX's collectives and lax.ppermute only.
A program may use at most 128 MiB of HBM per device.

```python
import jax
import jax.numpy as jnp
from jax import lax

D = 768
HEADS = 12
HEAD_DIM = 64
FF = 3072
BUCKETS = 32
LENGTH = 512
EXPERTS = 16
TOK_DEV = 512
TOKENS = 8192
CAP = 40
N_MP = 2


def route_draw(key):
    base = jax.random.fold_in(key, 11)
    block_count = TOKENS // TOK_DEV
    pair_count = EXPERTS * CAP
    common_full = jax.random.randint(jax.random.fold_in(base, 1), (), 0, EXPERTS)
    block_order = jax.random.permutation(jax.random.fold_in(base, 2), block_count).astype(jnp.int32)
    block_keys = jax.random.split(jax.random.fold_in(base, 3), block_count)
    pair_index = jnp.arange(pair_count, dtype=jnp.int32)
    pair_expert = pair_index // CAP
    pair_slot = pair_index % CAP

    def one_block(block_key, block_rank):
        first_key, second_key = jax.random.split(block_key)
        shuffled = jax.random.permutation(first_key, pair_count).astype(jnp.int32)
        second_full = (common_full + 1 + block_rank) % EXPERTS
        priority = jnp.where(pair_expert == common_full, pair_slot, jnp.where(pair_expert == second_full, CAP + pair_slot, 2 * CAP + shuffled))
        taken = jnp.argsort(priority)[:TOK_DEV]
        placed = taken[jax.random.permutation(second_key, TOK_DEV)]
        return (pair_expert[placed], pair_slot[placed])
    experts_drawn, slots_drawn = jax.vmap(one_block)(block_keys, block_order)
    return (experts_drawn.reshape(TOKENS).astype(jnp.int32), slots_drawn.reshape(TOKENS).astype(jnp.int32))


def draw_expert_ids(key, part):
    return route_draw(key)[0]


def draw_slot_ids(key, part):
    return route_draw(key)[1]


def draw_bucket_ids(key, part):
    base = jax.random.fold_in(key, 23)
    quarter = BUCKETS // 4
    half_count = BUCKETS // 2
    limits = quarter + jax.random.randint(base, (2, quarter - 1), 0, LENGTH - quarter)
    positions = jnp.arange(LENGTH, dtype=jnp.int32)
    offset = positions[None, :] - positions[:, None]
    distance = jnp.abs(offset)
    after = (offset > 0).astype(jnp.int32)
    side_limits = limits[after]
    far_bucket = quarter + jnp.sum((distance[:, :, None] >= side_limits).astype(jnp.int32), axis=-1)
    within = jnp.where(distance < quarter, distance, far_bucket)
    return (after * half_count + jnp.minimum(within, half_count - 1)).astype(jnp.int32)


def block_levels(rng, extent, pieces, least, top_value):
    def one(dim, blocks):
        steps = jax.random.uniform(jax.random.fold_in(jax.random.fold_in(rng, 6), dim), (blocks,), jnp.float32, least / len(pieces), top_value / len(pieces))
        return jnp.repeat(jnp.exp(steps), extent[dim] // blocks).reshape((-1,) + (1,) * (len(extent) - dim - 1))

    level = one(*pieces[0])
    for cut in pieces[1:]:
        level = level * one(*cut)
    return level


def noise(key, dims, scale, limit, pieces=(), kind=jnp.bfloat16):
    drawn = scale * jax.random.normal(key, dims, jnp.float32)
    if pieces:
        drawn = drawn * block_levels(key, dims, pieces, -0.22, 0.18)
    return jnp.clip(drawn, -limit, limit).astype(kind)


def setup_inputs(seed: int = 0) -> dict:
    keys = jax.random.split(jax.random.key(seed), 16)
    return {
        "hidden_in": noise(keys[0], (TOKENS, D), 1.0, 6.0, ((0, 16),)),
        "norm1_gain": jnp.clip(1.0 + 0.1 * jax.random.normal(keys[1], (D,), jnp.float32), 0.5, 1.5),
        "w_query": noise(keys[2], (D, D), (D // 2) ** -0.5, 0.3125, ((1, 2),)),
        "w_key": noise(keys[3], (D, D), D ** -0.5, 0.21875, ((1, 2),)),
        "w_value": noise(keys[4], (D, D), D ** -0.5, 0.21875, ((1, 2),)),
        "w_output": noise(keys[5], (D, D), (D // 32) ** -0.5, 1.25, ((0, 2),)),
        "bias_table": noise(keys[6], (BUCKETS, HEADS), 1.0, 4.0, ((1, 2),), jnp.float32),
        "bucket_ids": draw_bucket_ids(jax.random.fold_in(keys[15], 71), 0),
        "norm2_gain": jnp.clip(1.0 + 0.1 * jax.random.normal(keys[8], (D,), jnp.float32), 0.5, 1.5),
        "router": noise(keys[9], (D, EXPERTS), (4 * D) ** -0.5, 0.109375, (), jnp.float32),
        "w_in": noise(keys[10], (EXPERTS, D, FF), D ** -0.5, 0.21875, ((0, 16), (2, 2))),
        "w_out": noise(keys[11], (EXPERTS, FF, D), (EXPERTS * (FF ** -0.5)), 1.75, ((0, 16), (1, 2))),
        "expert_ids": draw_expert_ids(jax.random.fold_in(keys[15], 71), 0),
        "slot_ids": draw_slot_ids(jax.random.fold_in(keys[15], 71), 0),
        "out_grad": noise(keys[14], (TOKENS, D), 1.0, 6.0, ((0, 16),)),
    }


@jax.custom_vjp
def low(v):
    return lax.optimization_barrier(v.astype(jnp.bfloat16)).astype(jnp.float32)

@jax.custom_vjp
def low_back(v):
    return v

def low_keep(v):
    return (low(v), None)

def low_pass(kept, grad):
    return (grad,)

def back_keep(v):
    return (v, None)

def back_low(kept, grad):
    return (low(grad),)
low.defvjp(low_keep, low_pass)
low_back.defvjp(back_keep, back_low)
epsilon = 1e-06
highest = lax.Precision.HIGHEST

def rms_norm(values, gain):
    return values * lax.rsqrt(lax.optimization_barrier(jnp.mean(values * values, axis=-1, keepdims=True)) + epsilon) * gain

def reference(hidden_in, norm1_gain, w_query, w_key, w_value, w_output, bias_table, bucket_ids, norm2_gain, router, w_in, w_out, expert_ids, slot_ids, out_grad):
    hidden_half = FF // N_MP
    block_count = TOKENS // TOK_DEV
    seq_count = TOKENS // LENGTH
    score_scale = HEAD_DIM ** (-0.5)
    bucket_table = (bucket_ids[:, :, None] == jnp.arange(BUCKETS, dtype=jnp.int32)[None, None, :]).astype(jnp.float32)
    token_block = jnp.arange(TOKENS, dtype=jnp.int32) // TOK_DEV
    flat_index = ((expert_ids * block_count + token_block) * CAP + slot_ids).astype(jnp.int32)

    def split_heads(matrix):
        return matrix.reshape(seq_count, LENGTH, HEADS, HEAD_DIM)

    def forward(inputs, gain_one, query_w, key_w, value_w, output_w, table, gain_two, router_w, in_w, out_w):
        normed1_low = low(rms_norm(inputs, gain_one))
        queries = low(low_back(jnp.dot(normed1_low, query_w, precision=highest)))
        keys_low = low(low_back(jnp.dot(normed1_low, key_w, precision=highest)))
        values_low = low(low_back(jnp.dot(normed1_low, value_w, precision=highest)))
        bias_map = jnp.einsum('ijb,bh->hij', bucket_table, table, precision=highest)

        def one_sequence(packed):
            query_seq, key_seq, value_seq = packed
            scores = low_back(jnp.einsum('qhd,khd->hqk', query_seq, key_seq, precision=highest) * score_scale + bias_map)
            weights = low(jax.nn.softmax(scores, axis=-1))
            attended = jnp.einsum('hqk,khd->qhd', weights, value_seq, precision=highest)
            return attended.reshape(LENGTH, D)
        attended = lax.map(jax.checkpoint(one_sequence), (split_heads(queries), split_heads(keys_low), split_heads(values_low))).reshape(TOKENS, D)
        attended_low = low(low_back(attended))
        attention = jnp.dot(attended_low, output_w, precision=highest)
        residual_mid = inputs + low_back(attention)
        normed2 = rms_norm(residual_mid, gain_two)
        expert_probs = jax.nn.softmax(jnp.dot(normed2, router_w, precision=highest), axis=-1)
        gate_prob = jnp.take_along_axis(expert_probs, expert_ids[:, None], axis=1)[:, 0]
        normed2_low = low(normed2)
        dispatch_buffer = jnp.zeros((EXPERTS * block_count * CAP, D), jnp.float32).at[flat_index].add(normed2_low)

        def one_expert(packed):
            expert_rows, weight_in, weight_out = packed
            summed = jnp.zeros((block_count * CAP, D), jnp.float32)
            for half_index in range(N_MP):
                first = half_index * hidden_half
                rows_here = low_back(expert_rows)
                hidden = low(low_back(jax.nn.gelu(jnp.dot(rows_here, weight_in[:, first:first + hidden_half], precision=highest))))
                summed = summed + jnp.dot(hidden, weight_out[first:first + hidden_half, :], precision=highest)
            return low(low_back(summed))
        expert_out = lax.map(jax.checkpoint(one_expert), (dispatch_buffer.reshape(EXPERTS, block_count * CAP, D), in_w, out_w)).reshape(EXPERTS * block_count * CAP, D)
        picked = expert_out[flat_index]
        return residual_mid + gate_prob[:, None] * picked
    float_args = tuple((argument.astype(jnp.float32) for argument in (hidden_in, norm1_gain, w_query, w_key, w_value, w_output, bias_table, norm2_gain, router, w_in, w_out)))
    output, pullback = jax.vjp(forward, *float_args)
    grads = pullback(out_grad.astype(jnp.float32))
    return (output.astype(jnp.bfloat16), grads[0], grads[1], grads[2], grads[3], grads[4], grads[5], grads[6], grads[7], grads[8], grads[9], grads[10])
```

```python
import functools

import jax
import jax.numpy as jnp
from jax import lax
from jax.experimental import pallas as pl
from jax.experimental.pallas import tpu as pltpu
from jax.sharding import PartitionSpec as P

epsilon = 1e-06
bf16 = jnp.bfloat16
f32 = jnp.float32
vmem_bytes = 48 * 1024 * 1024
gelu_scale = 0.7978845608028654
gelu_cubic = 0.044715


def dot(left, right):
    return jnp.dot(left, right, preferred_element_type=f32)


def contract_last(left, right):
    return lax.dot_general(left, right, (((1,), (1,)), ((), ())), preferred_element_type=f32)


def contract_rows(left, right, precision=None):
    return lax.dot_general(
        left, right, (((0,), (0,)), ((), ())), preferred_element_type=f32, precision=precision
    )


def whole(shape):
    return pl.BlockSpec(shape, lambda *_: (0,) * len(shape))


def scalars():
    return pl.BlockSpec(memory_space=pltpu.SMEM)


def params():
    return pltpu.CompilerParams(vmem_limit_bytes=vmem_bytes)


def cost(flops, moved):
    return pl.CostEstimate(flops=flops, bytes_accessed=moved, transcendentals=0)


def attend_kernel(
    x_ref, gain_ref, wq_ref, wk_ref, wv_ref, table_ref, bucket_ref,
    o_ref, q_ref, k_ref, v_ref, p_ref, n_ref, bias_ref,
):
    pair = pl.program_id(0)
    length = x_ref.shape[0]
    buckets = table_ref.shape[0]
    half = o_ref.shape[1] // 2
    scale = half ** (-0.5)
    blocks = length // 128

    @pl.when(pair == 0)
    def _():
        x = x_ref[...].astype(f32)
        inverse = lax.rsqrt(jnp.mean(x * x, axis=-1, keepdims=True) + epsilon)
        n_ref[...] = (x * inverse * gain_ref[...]).astype(bf16)

    normed = n_ref[...]
    q = dot(normed, wq_ref[...]).astype(bf16)
    k = dot(normed, wk_ref[...]).astype(bf16)
    v = dot(normed, wv_ref[...]).astype(bf16)
    q_ref[...] = q
    k_ref[...] = k
    v_ref[...] = v
    ids = bucket_ref[...]
    lane = lax.broadcasted_iota(jnp.int32, (length, 2 * half), 1)
    zero = jnp.zeros_like(q)
    out = None
    for h in range(2):
        head = 2 * pair + h
        mine = (lane < half) if h == 0 else (lane >= half)
        spread = jnp.zeros(ids.shape, f32)
        for b in range(buckets):
            spread = jnp.where(ids == b, table_ref[b, head], spread)
        for a in range(16):
            left = 127 - 8 * a
            bias_ref[8 * a : 8 * a + 8, :] = pltpu.roll(spread, 2 * length - left, 1)
        q_head = jnp.where(mine, q, zero)
        for i in range(blocks):
            rows = slice(128 * i, 128 * i + 128)
            start = 128 * (blocks - 1 - i)
            s = contract_last(q_head[rows], k) * scale + bias_ref[:, start : start + length]
            e = jnp.exp(s - jnp.max(s, axis=-1, keepdims=True))
            p = e / jnp.sum(e, axis=-1, keepdims=True)
            p_ref[h, rows, :] = p.astype(bf16)
        part = dot(p_ref[h], jnp.where(mine, v, zero))
        out = part if out is None else out + part
    o_ref[...] = out.astype(bf16)


def attend(x, gain, wq, wk, wv, table, ids):
    length, width = x.shape
    local = wq.shape[1]
    heads = table.shape[1]
    span = 2 * local // heads
    column = pl.BlockSpec((length, span), lambda j: (0, j))
    weight = pl.BlockSpec((width, span), lambda j: (0, j))
    thin = jax.ShapeDtypeStruct((length, local), bf16)
    return pl.pallas_call(
        attend_kernel,
        grid=(heads // 2,),
        in_specs=[
            whole((length, width)), whole((1, width)), weight, weight, weight, scalars(),
            whole(ids.shape),
        ],
        out_specs=[
            column, column, column, column,
            pl.BlockSpec((2, length, length), lambda j: (j, 0, 0)),
            whole((length, width)),
        ],
        out_shape=[
            thin, thin, thin, thin,
            jax.ShapeDtypeStruct((heads, length, length), bf16),
            jax.ShapeDtypeStruct((length, width), bf16),
        ],
        scratch_shapes=[pltpu.VMEM((128, 2 * length), f32)],
        compiler_params=params(),
        cost_estimate=cost(2_000_000_000, 9_000_000),
        name="attend",
    )(x, gain, wq, wk, wv, table, ids)


def attend_back_kernel(
    do_ref, q_ref, k_ref, v_ref, p_ref, wq_ref, wk_ref, wv_ref,
    dq_ref, dk_ref, dv_ref, diag_ref, dn_ref, ds_ref, acc_ref, total_ref,
):
    pair = pl.program_id(0)
    length = do_ref.shape[0]
    half = do_ref.shape[1] // 2
    scale = half ** (-0.5)
    blocks = length // 128
    do = do_ref[...]
    q = q_ref[...]
    k = k_ref[...]
    v = v_ref[...]
    q_turned = q.T
    do_turned = do.T
    lane = lax.broadcasted_iota(jnp.int32, (length, 2 * half), 1)
    zero = jnp.zeros_like(q)
    dq = None
    dk_parts = []
    dv_parts = []
    for h in range(2):
        mine = (lane < half) if h == 0 else (lane >= half)
        do_head = jnp.where(mine, do, zero)
        acc_ref[...] = jnp.zeros_like(acc_ref)
        for i in range(blocks):
            rows = slice(128 * i, 128 * i + 128)
            start = 128 * (blocks - 1 - i)
            p = p_ref[h, rows, :].astype(f32)
            dp = contract_last(do_head[rows], v)
            ds = p * (dp - jnp.sum(p * dp, axis=-1, keepdims=True))
            acc_ref[:, start : start + length] += ds
            ds_ref[rows, :] = ds.astype(bf16)
        ds_all = ds_ref[...]
        part = dot(ds_all, jnp.where(mine, k, zero))
        dq = part if dq is None else dq + part
        dk_parts.append(dot(q_turned[h * half : (h + 1) * half], ds_all))
        dv_parts.append(dot(do_turned[h * half : (h + 1) * half], p_ref[h]))
        diag = None
        for a in range(16):
            piece = pltpu.roll(acc_ref[8 * a : 8 * a + 8, :], 127 - 8 * a, 1)
            diag = piece if diag is None else diag + piece
        diag_ref[h] = diag
    dq_low = (dq * scale).astype(bf16)
    dk_low = (jnp.concatenate(dk_parts, axis=0) * scale).T.astype(bf16)
    dv_low = jnp.concatenate(dv_parts, axis=0).T.astype(bf16)
    dq_ref[...] = dq_low
    dk_ref[...] = dk_low
    dv_ref[...] = dv_low
    part = (
        contract_last(dq_low, wq_ref[...])
        + contract_last(dk_low, wk_ref[...])
        + contract_last(dv_low, wv_ref[...])
    )

    @pl.when(pair == 0)
    def _():
        total_ref[...] = part

    @pl.when(pair > 0)
    def _():
        total_ref[...] += part

    @pl.when(pair == pl.num_programs(0) - 1)
    def _():
        dn_ref[...] = total_ref[...].astype(bf16)


def attend_back(do, q, k, v, p, wq, wk, wv):
    length, local = do.shape
    width = wq.shape[0]
    heads = p.shape[0]
    span = 2 * local // heads
    column = pl.BlockSpec((length, span), lambda j: (0, j))
    weight = pl.BlockSpec((width, span), lambda j: (0, j))
    thin = jax.ShapeDtypeStruct((length, local), bf16)
    return pl.pallas_call(
        attend_back_kernel,
        grid=(heads // 2,),
        in_specs=[
            column, column, column, column,
            pl.BlockSpec((2, length, length), lambda j: (j, 0, 0)),
            weight, weight, weight,
        ],
        out_specs=[
            column, column, column,
            pl.BlockSpec((2, 8, 2 * length), lambda j: (j, 0, 0)),
            whole((length, width)),
        ],
        out_shape=[
            thin, thin, thin,
            jax.ShapeDtypeStruct((heads, 8, 2 * length), f32),
            jax.ShapeDtypeStruct((length, width), bf16),
        ],
        scratch_shapes=[
            pltpu.VMEM((length, length), bf16),
            pltpu.VMEM((128, 2 * length), f32),
            pltpu.VMEM((length, width), f32),
        ],
        compiler_params=params(),
        cost_estimate=cost(3_000_000_000, 9_000_000),
        name="attend_back",
    )(do, q, k, v, p, wq, wk, wv)


def expert_kernel(
    x_ref, c_ref, w_in_ref, w_out_ref, router_ref, mine_ref,
    dx_ref, hid_ref, dpre_ref, deo_ref, gate_ref, dlog_ref,
    pre_ref, up_ref, probs_ref, inner_ref, total_ref,
):
    step = pl.program_id(0)
    rows = x_ref.shape[0]
    chunk = 64
    hot = lax.broadcasted_iota(jnp.int32, probs_ref.shape, 1) == mine_ref[0]

    @pl.when(step == 0)
    def _():
        router = router_ref[...]
        high = router.astype(bf16)
        rest = (router - high.astype(f32)).astype(bf16)
        logits = dot(x_ref[...], high) + dot(x_ref[...], rest)
        e = jnp.exp(logits - jnp.max(logits, axis=-1, keepdims=True))
        probs = e / jnp.sum(e, axis=-1, keepdims=True)
        gate = jnp.sum(jnp.where(hot, probs, 0.0), axis=-1, keepdims=True)
        probs_ref[...] = probs
        gate_ref[...] = gate
        deo_ref[...] = (gate * c_ref[...].astype(f32)).astype(bf16)

    pre_ref[...] = dot(x_ref[...], w_in_ref[...])
    up_ref[...] = contract_last(deo_ref[...], w_out_ref[...])
    for r in range(0, rows, chunk):
        part = slice(r, r + chunk)
        u = pre_ref[part, :]
        up = up_ref[part, :]
        square = u * u
        t = jnp.tanh(gelu_scale * u * (1.0 + gelu_cubic * square))
        side = 0.5 * (1.0 + t)
        hid = u * side
        slope = side + (0.5 * gelu_scale) * u * (1.0 - t * t) * (1.0 + (3.0 * gelu_cubic) * square)
        hid_ref[part, :] = hid.astype(bf16)
        dpre_ref[part, :] = (up * slope).astype(bf16)
        inner = jnp.sum(hid * up, axis=-1, keepdims=True)
        before = jnp.where(step == 0, 0.0, inner_ref[part, :])
        inner_ref[part, :] = before + inner
    part = contract_last(dpre_ref[...], w_in_ref[...])

    @pl.when(step == 0)
    def _():
        total_ref[...] = part

    @pl.when(step > 0)
    def _():
        total_ref[...] += part

    @pl.when(step == pl.num_programs(0) - 1)
    def _():
        dlog = inner_ref[...] * (hot.astype(f32) - probs_ref[...])
        dlog_ref[...] = dlog
        dx_ref[...] = (
            total_ref[...] + contract_last(dlog.astype(bf16), router_ref[...].astype(bf16))
        ).astype(bf16)


def expert(x, c, w_in, w_out, router, mine):
    rows, width = x.shape
    hidden = w_in.shape[1]
    experts = router.shape[1]
    step = 512 if hidden % 512 == 0 else hidden
    return pl.pallas_call(
        expert_kernel,
        grid=(hidden // step,),
        in_specs=[
            whole((rows, width)), whole((rows, width)),
            pl.BlockSpec((width, step), lambda j: (0, j)),
            pl.BlockSpec((step, width), lambda j: (j, 0)),
            whole((width, experts)), scalars(),
        ],
        out_specs=[
            whole((rows, width)),
            pl.BlockSpec((rows, step), lambda j: (0, j)),
            pl.BlockSpec((rows, step), lambda j: (0, j)),
            whole((rows, width)), whole((rows, 1)), whole((rows, experts)),
        ],
        out_shape=[
            jax.ShapeDtypeStruct((rows, width), bf16),
            jax.ShapeDtypeStruct((rows, hidden), bf16),
            jax.ShapeDtypeStruct((rows, hidden), bf16),
            jax.ShapeDtypeStruct((rows, width), bf16),
            jax.ShapeDtypeStruct((rows, 1), f32),
            jax.ShapeDtypeStruct((rows, experts), f32),
        ],
        scratch_shapes=[
            pltpu.VMEM((rows, step), f32),
            pltpu.VMEM((rows, step), f32),
            pltpu.VMEM((rows, experts), f32),
            pltpu.VMEM((rows, 1), f32),
            pltpu.VMEM((rows, width), f32),
        ],
        compiler_params=params(),
        cost_estimate=cost(4_500_000_000, 12_000_000),
        name="expert",
    )(x, c, w_in, w_out, router, mine)


def pair_list(count, bit):
    return [(i, i ^ (1 << bit)) for i in range(count)]


def scatter_step(value, count, bit):
    side = (lax.axis_index("dp") >> bit) & 1
    n = value.shape[0] // 2
    first, second = value[:n], value[n:]
    keep = jnp.where(side == 0, first, second)
    send = jnp.where(side == 0, second, first)
    got = lax.ppermute(send, "dp", pair_list(count, bit))
    return (keep.astype(f32) + got.astype(f32)).astype(value.dtype)


def gather_step(value, count, bit):
    side = (lax.axis_index("dp") >> bit) & 1
    got = lax.ppermute(value, "dp", pair_list(count, bit))
    return jnp.concatenate(
        [jnp.where(side == 0, value, got), jnp.where(side == 0, got, value)]
    )


def dp_sum(value, count, order):
    for bit in order:
        value = scatter_step(value, count, bit)
    for bit in order[::-1]:
        value = gather_step(value, count, bit)
    return value


def shards(
    count,
    hidden_in,
    norm1_gain,
    w_query,
    w_key,
    w_value,
    w_output,
    bias_table,
    bucket_ids,
    norm2_gain,
    router,
    w_in,
    w_out,
    expert_ids,
    slot_ids,
    out_grad,
):
    tokens, width = hidden_in.shape
    buckets, heads = bias_table.shape
    length = bucket_ids.shape[0]
    experts = router.shape[1]
    capacity = max(2, 5 * tokens // (4 * experts))
    places = experts * capacity
    bits = (count - 1).bit_length()
    order_a = tuple(range(bits))
    order_b = (0, 2, 1) + tuple(range(3, bits))
    swap = [(0, 1), (1, 0)]
    mp = lax.axis_index("mp")
    dp = lax.axis_index("dp")

    def swapped(value):
        return lax.ppermute(value, "mp", swap)

    def to_experts(rows):
        block = rows.reshape(experts, capacity, width)
        return lax.all_to_all(block, "dp", split_axis=0, concat_axis=0, tiled=True).reshape(
            places, width
        )

    flat_slot = expert_ids * capacity + slot_ids
    table = (jnp.arange(places, dtype=jnp.int32)[:, None] == flat_slot[None, :]).astype(bf16)

    c_here = to_experts(dot(table, out_grad).astype(bf16))
    w_output_other = swapped(w_output)

    line = jnp.concatenate(
        [
            jnp.zeros((8,), jnp.int32), bucket_ids[length - 1], bucket_ids[0, 1:],
            jnp.zeros((1,), jnp.int32),
        ]
    )
    offsets = jnp.stack([line[8 - r : 8 - r + 2 * length] for r in range(8)])

    o, q, k, v, p, normed1 = attend(
        hidden_in, norm1_gain[None, :], w_query, w_key, w_value, bias_table, offsets
    )
    o_other = swapped(o)
    low = mp == 0
    o_all = jnp.concatenate([jnp.where(low, o, o_other), jnp.where(low, o_other, o)], axis=1)
    w_all = jnp.concatenate(
        [jnp.where(low, w_output, w_output_other), jnp.where(low, w_output_other, w_output)]
    )
    hmid = hidden_in.astype(f32) + dot(o_all, w_all)
    inverse2 = lax.rsqrt(jnp.mean(hmid * hmid, axis=-1, keepdims=True) + epsilon)
    normed2 = (hmid * inverse2 * norm2_gain).astype(bf16)
    x_here = to_experts(dot(table, normed2).astype(bf16))

    dx, hid, dpre, deo, gate, dlog = expert(
        x_here, c_here, w_in[0], w_out[0], router, dp.astype(jnp.int32)[None]
    )
    dx_home = to_experts(dx)
    eo = (gate * dot(hid, w_out[0])).astype(bf16)
    eo = (eo.astype(f32) + swapped(eo).astype(f32)).astype(bf16)
    grad_w_out = contract_rows(hid, deo)[None]
    grad_w_in = contract_rows(x_here, dpre)[None]
    grad_router = contract_rows(x_here.astype(f32), dlog, lax.Precision.HIGHEST)
    grad_router = grad_router + swapped(grad_router)
    eo_home = to_experts(eo)

    dn2 = contract_rows(table, dx_home).astype(bf16)
    dn2 = dn2.astype(f32) + swapped(dn2).astype(f32)
    c = out_grad.astype(f32)
    scaled = dn2 * norm2_gain
    dh = c + inverse2 * scaled - hmid * inverse2**3 * jnp.mean(scaled * hmid, axis=-1, keepdims=True)
    grad_norm2 = jnp.sum(dn2 * hmid * inverse2, axis=0)
    da = dh.astype(bf16)
    do = contract_last(da, w_output).astype(bf16)
    grad_w_output = contract_rows(o, da).astype(bf16)
    hidden_out = (hmid + contract_rows(table, eo_home)).astype(bf16)

    dq, dk, dv, diag, dn1 = attend_back(do, q, k, v, p, w_query, w_key, w_value)
    x = hidden_in.astype(f32)
    inverse1 = lax.rsqrt(jnp.mean(x * x, axis=-1, keepdims=True) + epsilon)
    grad_norm1 = jnp.sum(dn1.astype(f32) * x * inverse1, axis=0)
    grad_norm1 = grad_norm1 + swapped(grad_norm1)
    dn1 = dn1.astype(f32) + swapped(dn1).astype(f32)
    scaled = dn1 * norm1_gain
    grad_hidden = dh + inverse1 * scaled - x * inverse1**3 * jnp.mean(
        scaled * x, axis=-1, keepdims=True
    )
    grad_table = jnp.einsum(
        "hrx,rxb->bh",
        diag,
        (offsets[:, :, None] == jnp.arange(buckets, dtype=jnp.int32)).astype(f32),
        precision=lax.Precision.HIGHEST,
    )
    small = jnp.concatenate(
        [
            grad_router,
            grad_norm1[:, None],
            grad_norm2[:, None],
            jnp.pad(grad_table.reshape(-1), (0, width - buckets * heads))[:, None],
            jnp.zeros((width, 128 - (experts + 3) % 128), f32),
        ],
        axis=1,
    ).astype(bf16)
    grad_q = contract_rows(normed1, dq).astype(bf16)
    grad_k = contract_rows(normed1, dk).astype(bf16)
    grad_v = contract_rows(normed1, dv).astype(bf16)
    grad_w_output = dp_sum(grad_w_output, count, order_b)
    kv = dp_sum(jnp.concatenate([grad_k, grad_v], axis=1), count, order_a)
    rest = dp_sum(jnp.concatenate([grad_q, small], axis=1), count, order_b)
    local = grad_q.shape[1]
    small = rest[:, local:].astype(f32)
    return (
        hidden_out,
        grad_hidden,
        small[:, experts],
        rest[:, :local].astype(f32),
        kv[:, :local].astype(f32),
        kv[:, local:].astype(f32),
        grad_w_output.astype(f32),
        small[: buckets * heads, experts + 2].reshape(buckets, heads),
        small[:, experts + 1],
        small[:, :experts],
        grad_w_in,
        grad_w_out,
    )


def solution(mesh):
    return jax.shard_map(
        functools.partial(shards, mesh.shape["dp"]),
        mesh=mesh,
        in_specs=(
            P("dp", None),
            P(),
            P(None, "mp"),
            P(None, "mp"),
            P(None, "mp"),
            P("mp", None),
            P(None, "mp"),
            P(),
            P(),
            P(),
            P("dp", None, "mp"),
            P("dp", "mp", None),
            P("dp"),
            P("dp"),
            P("dp", None),
        ),
        out_specs=(
            P("dp", None),
            P("dp", None),
            P(),
            P(None, "mp"),
            P(None, "mp"),
            P(None, "mp"),
            P("mp", None),
            P(None, "mp"),
            P(),
            P(),
            P("dp", None, "mp"),
            P("dp", "mp", None),
        ),
        check_vma=False,
    )
```

```python
import functools

import jax
import jax.numpy as jnp
from jax import lax
from jax.experimental import pallas as pl
from jax.experimental.pallas import tpu as pltpu
from jax.sharding import PartitionSpec as P

epsilon = 1e-06
bf16 = jnp.bfloat16
f32 = jnp.float32
vmem_bytes = 62 * 1024 * 1024
gelu_scale = 0.7978845608028654
gelu_cubic = 0.044715


def dot(left, right):
    return jnp.dot(left, right, preferred_element_type=f32)


def contract_last(left, right):
    return lax.dot_general(left, right, (((1,), (1,)), ((), ())), preferred_element_type=f32)


def contract_rows(left, right, precision=None):
    return lax.dot_general(
        left, right, (((0,), (0,)), ((), ())), preferred_element_type=f32, precision=precision
    )


def whole(shape):
    return pl.BlockSpec(shape, lambda *_: (0,) * len(shape))


def scalars():
    return pl.BlockSpec(memory_space=pltpu.SMEM)


def params():
    return pltpu.CompilerParams(vmem_limit_bytes=vmem_bytes)


def cost(flops, moved):
    return pl.CostEstimate(flops=flops, bytes_accessed=moved, transcendentals=0)


def attend_kernel(
    x_ref, gain_ref, wq_ref, wk_ref, wv_ref, table_ref, first_ref, last_ref,
    o_ref, q_ref, k_ref, v_ref, p_ref, ids_ref, n_ref, bias_ref,
):
    pair = pl.program_id(0)
    length = x_ref.shape[0]
    buckets = table_ref.shape[0]
    half = o_ref.shape[1] // 2
    scale = half ** (-0.5)
    blocks = length // 128

    @pl.when(pair == 0)
    def _():
        x = x_ref[...].astype(f32)
        inverse = lax.rsqrt(jnp.mean(x * x, axis=-1, keepdims=True) + epsilon)
        n_ref[...] = (x * inverse * gain_ref[...]).astype(bf16)
        blank = jnp.zeros((8, length), jnp.int32)
        ahead = jnp.concatenate([jnp.broadcast_to(first_ref[0:1, :], (8, length)), blank], axis=1)
        behind = jnp.concatenate([jnp.broadcast_to(last_ref[7:8, :], (8, length)), blank], axis=1)
        place = lax.broadcasted_iota(jnp.int32, (8, 2 * length), 1)
        row = lax.broadcasted_iota(jnp.int32, (8, 2 * length), 0)
        line = jnp.where(place < length, behind, pltpu.roll(ahead, length - 1, 1))
        ids = line
        for r in range(1, 8):
            ids = jnp.where(row == r, pltpu.roll(line, r, 1), ids)
        ids_ref[...] = ids

    normed = n_ref[...]
    q = dot(normed, wq_ref[...]).astype(bf16)
    k = dot(normed, wk_ref[...]).astype(bf16)
    v = dot(normed, wv_ref[...]).astype(bf16)
    q_ref[...] = q
    k_ref[...] = k
    v_ref[...] = v
    ids = ids_ref[...]
    lane = lax.broadcasted_iota(jnp.int32, (length, 2 * half), 1)
    zero = jnp.zeros_like(q)
    out = None
    for h in range(2):
        head = 2 * pair + h
        mine = (lane < half) if h == 0 else (lane >= half)
        spread = jnp.zeros(ids.shape, f32)
        for b in range(buckets):
            spread = jnp.where(ids == b, table_ref[b, head], spread)
        for a in range(16):
            left = 127 - 8 * a
            bias_ref[8 * a : 8 * a + 8, :] = pltpu.roll(spread, 2 * length - left, 1)
        q_head = jnp.where(mine, q, zero)
        for i in range(blocks):
            rows = slice(128 * i, 128 * i + 128)
            start = 128 * (blocks - 1 - i)
            s = contract_last(q_head[rows], k) * scale + bias_ref[:, start : start + length]
            e = jnp.exp(s - jnp.max(s, axis=-1, keepdims=True))
            p = e / jnp.sum(e, axis=-1, keepdims=True)
            p_ref[h, rows, :] = p.astype(bf16)
        part = dot(p_ref[h], jnp.where(mine, v, zero))
        out = part if out is None else out + part
    o_ref[...] = out.astype(bf16)


def attend(x, gain, wq, wk, wv, table, bucket_ids):
    length, width = x.shape
    local = wq.shape[1]
    heads = table.shape[1]
    span = 2 * local // heads
    column = pl.BlockSpec((length, span), lambda j: (0, j))
    weight = pl.BlockSpec((width, span), lambda j: (0, j))
    thin = jax.ShapeDtypeStruct((length, local), bf16)
    return pl.pallas_call(
        attend_kernel,
        grid=(heads // 2,),
        in_specs=[
            whole((length, width)), whole((1, width)), weight, weight, weight, scalars(),
            pl.BlockSpec((8, length), lambda j: (0, 0)),
            pl.BlockSpec((8, length), lambda j: (length // 8 - 1, 0)),
        ],
        out_specs=[
            column, column, column, column,
            pl.BlockSpec((2, length, length), lambda j: (j, 0, 0)),
            whole((8, 2 * length)),
        ],
        out_shape=[
            thin, thin, thin, thin,
            jax.ShapeDtypeStruct((heads, length, length), bf16),
            jax.ShapeDtypeStruct((8, 2 * length), jnp.int32),
        ],
        scratch_shapes=[pltpu.VMEM((length, width), bf16), pltpu.VMEM((128, 2 * length), f32)],
        compiler_params=params(),
        cost_estimate=cost(9_000_000_000, 9_000_000),
        name="attend",
    )(x, gain, wq, wk, wv, table, bucket_ids, bucket_ids)


def attend_back_kernel(
    side_ref, do_ref, q_ref, k_ref, v_ref, p_ref, wq_ref, wk_ref, wv_ref,
    o_ref, da_ref, x_ref, gain_ref, ids_ref, router_ref, norm2_ref, buckets_ref,
    dn_ref, keep_a_ref, send_a_ref, keep_b_ref, send_b_ref,
    ds_ref, acc_ref, total_ref, n_ref, small_ref,
):
    pair = pl.program_id(0)
    last = pl.num_programs(0) - 1
    length = do_ref.shape[0]
    span = do_ref.shape[1]
    half = span // 2
    scale = half ** (-0.5)
    blocks = length // 128
    buckets = buckets_ref.shape[0]
    experts = router_ref.shape[0]
    local = keep_a_ref.shape[0]
    even = side_ref[0] == 0

    @pl.when(pair == 0)
    def _():
        x = x_ref[...].astype(f32)
        inverse = lax.rsqrt(jnp.mean(x * x, axis=-1, keepdims=True) + epsilon)
        n_ref[...] = (x * inverse * gain_ref[...]).astype(bf16)
        small_ref[...] = jnp.zeros_like(small_ref)
        small_ref[0:experts, :] = router_ref[...]
        small_ref[experts + 1 : experts + 2, :] = norm2_ref[...]

    do = do_ref[...]
    q = q_ref[...]
    k = k_ref[...]
    v = v_ref[...]
    ids = ids_ref[...]
    q_turned = q.T
    do_turned = do.T
    lane = lax.broadcasted_iota(jnp.int32, (length, span), 1)
    zero = jnp.zeros_like(q)
    dq = None
    dk_parts = []
    dv_parts = []
    for h in range(2):
        mine = (lane < half) if h == 0 else (lane >= half)
        do_head = jnp.where(mine, do, zero)
        acc_ref[...] = jnp.zeros_like(acc_ref)
        for i in range(blocks):
            rows = slice(128 * i, 128 * i + 128)
            start = 128 * (blocks - 1 - i)
            p = p_ref[h, rows, :].astype(f32)
            dp = contract_last(do_head[rows], v)
            ds = p * (dp - jnp.sum(p * dp, axis=-1, keepdims=True))
            acc_ref[:, start : start + length] += ds
            ds_ref[rows, :] = ds.astype(bf16)
        ds_all = ds_ref[...]
        part = dot(ds_all, jnp.where(mine, k, zero))
        dq = part if dq is None else dq + part
        dk_parts.append(dot(q_turned[h * half : (h + 1) * half], ds_all))
        dv_parts.append(dot(do_turned[h * half : (h + 1) * half], p_ref[h]))
        diag = None
        for a in range(16):
            piece = pltpu.roll(acc_ref[8 * a : 8 * a + 8, :], 127 - 8 * a, 1)
            diag = piece if diag is None else diag + piece
        lines = []
        for b in range(buckets):
            hit = jnp.where(ids == b, diag, 0.0)
            fold = hit[:, 0:128]
            for y in range(1, 2 * length // 128):
                fold = fold + hit[:, 128 * y : 128 * y + 128]
            lines.append(jnp.sum(fold, axis=0, keepdims=True))
        lines.append(jnp.zeros((128 - buckets, 128), f32))
        sums = jnp.sum(jnp.concatenate(lines, axis=0).T, axis=0, keepdims=True)
        row = lax.broadcasted_iota(jnp.int32, (small_ref.shape[0], 128), 0)
        small_ref[:, 0:128] = jnp.where(
            row == experts + 2 + 2 * pair + h, sums, small_ref[:, 0:128]
        )
    dq_low = (dq * scale).astype(bf16)
    dk_turned = (jnp.concatenate(dk_parts, axis=0) * scale).astype(bf16)
    dv_turned = jnp.concatenate(dv_parts, axis=0).astype(bf16)
    part = (
        contract_last(dq_low, wq_ref[...])
        + contract_last(dk_turned.T, wk_ref[...])
        + contract_last(dv_turned.T, wv_ref[...])
    )
    normed = n_ref[...]
    here = pl.ds(pl.multiple_of(pair * span, span), span)
    grad_k = dot(dk_turned, normed).astype(bf16)
    grad_v = dot(dv_turned, normed).astype(bf16)
    keep_a_ref[here, :] = jnp.where(even, grad_k, grad_v)
    send_a_ref[here, :] = jnp.where(even, grad_v, grad_k)
    grad_q = dot(dq_low.T, normed).astype(bf16)
    grad_o = dot(o_ref[...].T, da_ref[...]).astype(bf16)
    keep_b_ref[here, :] = jnp.where(even, grad_q, grad_o)
    send_b_ref[here, :] = jnp.where(even, grad_o, grad_q)

    @pl.when(pair == 0)
    def _():
        total_ref[...] = part

    @pl.when(pair > 0)
    def _():
        total_ref[...] += part

    @pl.when(pair == last)
    def _():
        total = total_ref[...]
        dn_ref[...] = total.astype(bf16)
        x = x_ref[...].astype(f32)
        inverse = lax.rsqrt(jnp.mean(x * x, axis=-1, keepdims=True) + epsilon)
        small_ref[experts : experts + 1, :] = jnp.sum(
            total * x * inverse, axis=0, keepdims=True
        )
        small = small_ref[...].astype(bf16)
        keep_b_ref[local:, :] = small
        send_b_ref[local:, :] = small


def small_rows(experts, heads):
    return -(-(experts + 2 + heads) // 64) * 64


def attend_back(side, do, q, k, v, p, wq, wk, wv, o, da, x, gain, ids, router, norm2, table):
    length, local = do.shape
    width = wq.shape[0]
    heads = p.shape[0]
    experts = router.shape[0]
    span = 2 * local // heads
    extra = small_rows(experts, heads)
    column = pl.BlockSpec((length, span), lambda j: (0, j))
    weight = pl.BlockSpec((width, span), lambda j: (0, j))
    part_a = jax.ShapeDtypeStruct((local, width), bf16)
    part_b = jax.ShapeDtypeStruct((local + extra, width), bf16)
    return pl.pallas_call(
        attend_back_kernel,
        grid=(heads // 2,),
        in_specs=[
            scalars(), column, column, column, column,
            pl.BlockSpec((2, length, length), lambda j: (j, 0, 0)),
            weight, weight, weight, column,
            whole((length, width)), whole((length, width)), whole((1, width)),
            whole(ids.shape), whole((experts, width)), whole((1, width)), whole(table.shape),
        ],
        out_specs=[
            whole((length, width)), whole(part_a.shape), whole(part_a.shape),
            whole(part_b.shape), whole(part_b.shape),
        ],
        out_shape=[
            jax.ShapeDtypeStruct((length, width), bf16), part_a, part_a, part_b, part_b,
        ],
        scratch_shapes=[
            pltpu.VMEM((length, length), bf16),
            pltpu.VMEM((128, 2 * length), f32),
            pltpu.VMEM((length, width), f32),
            pltpu.VMEM((length, width), bf16),
            pltpu.VMEM((extra, width), f32),
        ],
        compiler_params=params(),
        cost_estimate=cost(12_000_000_000, 9_000_000),
        name="attend_back",
    )(side, do, q, k, v, p, wq, wk, wv, o, da, x, gain, ids, router, norm2, table)


def hits(ids, count, axis):
    shape = (count, ids.shape[1]) if axis == 0 else (ids.shape[0], count)
    return jnp.where(lax.broadcasted_iota(jnp.int32, shape, axis) == ids, 1.0, 0.0).astype(bf16)


def place_kernel(ids_ref, rows_ref, out_ref):
    out_ref[...] = dot(hits(ids_ref[...], out_ref.shape[0], 0), rows_ref[...]).astype(bf16)


def place(ids, rows, places):
    return pl.pallas_call(
        place_kernel,
        out_shape=jax.ShapeDtypeStruct((places, rows.shape[1]), bf16),
        compiler_params=params(),
        cost_estimate=cost(1_000_000_000, 3_000_000),
        name="place",
    )(ids, rows)


def pick_kernel(ids_ref, slots_ref, out_ref):
    out_ref[...] = dot(hits(ids_ref[...], slots_ref.shape[0], 1), slots_ref[...]).astype(bf16)


def pick(ids, slots):
    return pl.pallas_call(
        pick_kernel,
        out_shape=jax.ShapeDtypeStruct((ids.shape[0], slots.shape[1]), bf16),
        compiler_params=params(),
        cost_estimate=cost(1_000_000_000, 3_000_000),
        name="pick",
    )(ids, slots)


def finish_kernel(own_ref, got_ref, hmid_ref, out_ref):
    picked = own_ref[...].astype(f32) + got_ref[...].astype(f32)
    out_ref[...] = (hmid_ref[...] + picked).astype(bf16)


def finish(own, got, hmid):
    return pl.pallas_call(
        finish_kernel,
        out_shape=jax.ShapeDtypeStruct(hmid.shape, bf16),
        compiler_params=params(),
        cost_estimate=cost(1_000_000, 5_000_000),
        name="finish",
    )(own, got, hmid)


def middle_kernel(
    mp_ref, o_ref, o_other_ref, w_ref, w_other_ref, x_ref, gain_ref, ids_ref, hmid_ref, out_ref
):
    low = mp_ref[0] == 0
    o, o_other = o_ref[...], o_other_ref[...]
    w, w_other = w_ref[...], w_other_ref[...]
    heads = jnp.concatenate([jnp.where(low, o, o_other), jnp.where(low, o_other, o)], axis=1)
    weight = jnp.concatenate([jnp.where(low, w, w_other), jnp.where(low, w_other, w)], axis=0)
    hmid = x_ref[...].astype(f32) + dot(heads, weight)
    hmid_ref[...] = hmid
    inverse = lax.rsqrt(jnp.mean(hmid * hmid, axis=-1, keepdims=True) + epsilon)
    normed = (hmid * inverse * gain_ref[...]).astype(bf16)
    out_ref[...] = dot(hits(ids_ref[...], out_ref.shape[0], 0), normed).astype(bf16)


def middle(mp, o, o_other, w, w_other, x, gain, ids, places):
    return pl.pallas_call(
        middle_kernel,
        in_specs=[scalars()] + [pl.BlockSpec(memory_space=pltpu.VMEM)] * 7,
        out_shape=[
            jax.ShapeDtypeStruct(x.shape, f32),
            jax.ShapeDtypeStruct((places, x.shape[1]), bf16),
        ],
        compiler_params=params(),
        cost_estimate=cost(2_000_000_000, 6_000_000),
        name="middle",
    )(mp, o, o_other, w, w_other, x, gain, ids)


def middle_back_kernel(
    own_ref, got_ref, hmid_ref, c_ref, gain_ref, w_ref, dh_ref, da_ref, do_ref, norm_ref
):
    hmid = hmid_ref[...]
    dn = own_ref[...].astype(f32) + got_ref[...].astype(f32)
    inverse = lax.rsqrt(jnp.mean(hmid * hmid, axis=-1, keepdims=True) + epsilon)
    scaled = dn * gain_ref[...]
    inner = jnp.mean(scaled * hmid, axis=-1, keepdims=True)
    dh = c_ref[...].astype(f32) + inverse * scaled - hmid * (inverse * inverse * inverse * inner)
    dh_ref[...] = dh
    da = dh.astype(bf16)
    da_ref[...] = da
    do_ref[...] = contract_last(da, w_ref[...]).astype(bf16)
    norm_ref[...] = jnp.sum(dn * hmid * inverse, axis=0, keepdims=True)


def middle_back(own, got, hmid, c, gain, w):
    tokens, width = own.shape
    return pl.pallas_call(
        middle_back_kernel,
        out_shape=[
            jax.ShapeDtypeStruct((tokens, width), f32),
            jax.ShapeDtypeStruct((tokens, width), bf16),
            jax.ShapeDtypeStruct((tokens, w.shape[0]), bf16),
            jax.ShapeDtypeStruct((1, width), f32),
        ],
        compiler_params=params(),
        cost_estimate=cost(1_000_000_000, 6_000_000),
        name="middle_back",
    )(own, got, hmid, c, gain, w)


def input_back_kernel(own_ref, got_ref, x_ref, dh_ref, gain_ref, out_ref):
    x = x_ref[...].astype(f32)
    dn = own_ref[...].astype(f32) + got_ref[...].astype(f32)
    inverse = lax.rsqrt(jnp.mean(x * x, axis=-1, keepdims=True) + epsilon)
    scaled = dn * gain_ref[...]
    inner = jnp.mean(scaled * x, axis=-1, keepdims=True)
    out_ref[...] = dh_ref[...] + inverse * scaled - x * (inverse * inverse * inverse * inner)


def input_back(own, got, x, dh, gain):
    return pl.pallas_call(
        input_back_kernel,
        out_shape=jax.ShapeDtypeStruct(dh.shape, f32),
        compiler_params=params(),
        cost_estimate=cost(100_000_000, 6_000_000),
        name="input_back",
    )(own, got, x, dh, gain)


def unpack_kernel(
    side_ref, a_ref, a_got_ref, b_ref, b_got_ref, s_got_ref,
    q_ref, k_ref, v_ref, o_ref, router_ref, table_ref, norm1_ref, norm2_ref,
):
    even = side_ref[0] == 0
    local, width = a_ref.shape
    experts = router_ref.shape[1]
    buckets, heads = table_ref.shape
    a, a_got = a_ref[...], a_got_ref[...]
    b, b_got = b_ref[0:local, :], b_got_ref[...]
    k_ref[...] = jnp.where(even, a, a_got).T.astype(f32)
    v_ref[...] = jnp.where(even, a_got, a).T.astype(f32)
    q_ref[...] = jnp.where(even, b, b_got).T.astype(f32)
    o_ref[...] = jnp.where(even, b_got, b).astype(f32)
    small = b_ref[local:, :].astype(f32)
    both = small + s_got_ref[...].astype(f32)
    pad = jnp.zeros((-small.shape[0] % 128, width), f32)
    router_ref[...] = jnp.concatenate([both, pad], axis=0).T[:, :experts]
    norm1_ref[...] = both[experts : experts + 1]
    norm2_ref[...] = small[experts + 1 : experts + 2]
    lines = small[experts + 2 : experts + 2 + heads, 0:128]
    pad = jnp.zeros((128 - heads, 128), f32)
    table_ref[...] = jnp.concatenate([lines, pad], axis=0).T[:buckets, :heads]


def unpack(side, a, a_got, b, b_got, s_got, experts, buckets, heads):
    local, width = a.shape
    turned = jax.ShapeDtypeStruct((width, local), f32)
    return pl.pallas_call(
        unpack_kernel,
        in_specs=[scalars()] + [pl.BlockSpec(memory_space=pltpu.VMEM)] * 5,
        out_shape=[
            turned, turned, turned,
            jax.ShapeDtypeStruct((local, width), f32),
            jax.ShapeDtypeStruct((width, experts), f32),
            jax.ShapeDtypeStruct((buckets, heads), f32),
            jax.ShapeDtypeStruct((1, width), f32),
            jax.ShapeDtypeStruct((1, width), f32),
        ],
        compiler_params=params(),
        cost_estimate=cost(100_000_000, 8_000_000),
        name="unpack",
    )(side, a, a_got, b, b_got, s_got)


def expert_kernel(
    x_ref, c_ref, w_in_ref, w_out_ref, router_ref, mine_ref,
    dx_ref, hid_ref, dpre_ref, deo_ref, gate_ref, dlog_ref,
    pre_ref, up_ref, probs_ref, inner_ref, total_ref,
):
    step = pl.program_id(0)
    rows = x_ref.shape[0]
    chunk = 64
    hot = lax.broadcasted_iota(jnp.int32, probs_ref.shape, 1) == mine_ref[0]

    @pl.when(step == 0)
    def _():
        router = router_ref[...]
        high = router.astype(bf16)
        rest = (router - high.astype(f32)).astype(bf16)
        logits = dot(x_ref[...], high) + dot(x_ref[...], rest)
        e = jnp.exp(logits - jnp.max(logits, axis=-1, keepdims=True))
        probs = e / jnp.sum(e, axis=-1, keepdims=True)
        gate = jnp.sum(jnp.where(hot, probs, 0.0), axis=-1, keepdims=True)
        probs_ref[...] = probs
        gate_ref[...] = gate
        deo_ref[...] = (gate * c_ref[...].astype(f32)).astype(bf16)

    pre_ref[...] = dot(x_ref[...], w_in_ref[...])
    up_ref[...] = contract_last(deo_ref[...], w_out_ref[...])
    for r in range(0, rows, chunk):
        part = slice(r, r + chunk)
        u = pre_ref[part, :]
        up = up_ref[part, :]
        square = u * u
        t = jnp.tanh(gelu_scale * u * (1.0 + gelu_cubic * square))
        side = 0.5 * (1.0 + t)
        hid = u * side
        slope = side + (0.5 * gelu_scale) * u * (1.0 - t * t) * (1.0 + (3.0 * gelu_cubic) * square)
        hid_ref[part, :] = hid.astype(bf16)
        dpre_ref[part, :] = (up * slope).astype(bf16)
        inner = jnp.sum(hid * up, axis=-1, keepdims=True)
        before = jnp.where(step == 0, 0.0, inner_ref[part, :])
        inner_ref[part, :] = before + inner
    part = contract_last(dpre_ref[...], w_in_ref[...])

    @pl.when(step == 0)
    def _():
        total_ref[...] = part

    @pl.when(step > 0)
    def _():
        total_ref[...] += part

    @pl.when(step == pl.num_programs(0) - 1)
    def _():
        dlog = inner_ref[...] * (hot.astype(f32) - probs_ref[...])
        dlog_ref[...] = dlog
        dx_ref[...] = (
            total_ref[...] + contract_last(dlog.astype(bf16), router_ref[...].astype(bf16))
        ).astype(bf16)


def expert(x, c, w_in, w_out, router, mine):
    rows, width = x.shape
    hidden = w_in.shape[1]
    experts = router.shape[1]
    step = 512 if hidden % 512 == 0 else hidden
    return pl.pallas_call(
        expert_kernel,
        grid=(hidden // step,),
        in_specs=[
            whole((rows, width)), whole((rows, width)),
            pl.BlockSpec((width, step), lambda j: (0, j)),
            pl.BlockSpec((step, width), lambda j: (j, 0)),
            whole((width, experts)), scalars(),
        ],
        out_specs=[
            whole((rows, width)),
            pl.BlockSpec((rows, step), lambda j: (0, j)),
            pl.BlockSpec((rows, step), lambda j: (0, j)),
            whole((rows, width)), whole((rows, 1)), whole((rows, experts)),
        ],
        out_shape=[
            jax.ShapeDtypeStruct((rows, width), bf16),
            jax.ShapeDtypeStruct((rows, hidden), bf16),
            jax.ShapeDtypeStruct((rows, hidden), bf16),
            jax.ShapeDtypeStruct((rows, width), bf16),
            jax.ShapeDtypeStruct((rows, 1), f32),
            jax.ShapeDtypeStruct((rows, experts), f32),
        ],
        scratch_shapes=[
            pltpu.VMEM((rows, step), f32),
            pltpu.VMEM((rows, step), f32),
            pltpu.VMEM((rows, experts), f32),
            pltpu.VMEM((rows, 1), f32),
            pltpu.VMEM((rows, width), f32),
        ],
        compiler_params=params(),
        cost_estimate=cost(4_500_000_000, 12_000_000),
        name="expert",
    )(x, c, w_in, w_out, router, mine)


def exchange(value, count, bit):
    return lax.ppermute(value, "dp", [(i, i ^ (1 << bit)) for i in range(count)])


def side_of(bit):
    return (lax.axis_index("dp") >> bit) & 1


def add(left, right):
    return (left.astype(f32) + right.astype(f32)).astype(left.dtype)


def halves(value, bit):
    n = value.shape[0] // 2
    first, second = value[:n], value[n:]
    low = side_of(bit) == 0
    return jnp.where(low, first, second), jnp.where(low, second, first)


def join(value, got, bit):
    low = side_of(bit) == 0
    return jnp.concatenate([jnp.where(low, value, got), jnp.where(low, got, value)])


def shards(
    count,
    hidden_in,
    norm1_gain,
    w_query,
    w_key,
    w_value,
    w_output,
    bias_table,
    bucket_ids,
    norm2_gain,
    router,
    w_in,
    w_out,
    expert_ids,
    slot_ids,
    out_grad,
):
    tokens, width = hidden_in.shape
    buckets, heads = bias_table.shape
    experts = router.shape[1]
    capacity = max(2, 5 * tokens // (4 * experts))
    places = experts * capacity
    bits = (count - 1).bit_length()
    swap = [(0, 1), (1, 0)]
    mp = lax.axis_index("mp").astype(jnp.int32)
    dp = lax.axis_index("dp").astype(jnp.int32)
    side = (dp & 1)[None]
    gain1 = norm1_gain[None, :]
    gain2 = norm2_gain[None, :]

    def swapped(value):
        return lax.ppermute(value, "mp", swap)

    def to_experts(rows):
        block = rows.reshape(experts, capacity, width)
        return lax.all_to_all(block, "dp", split_axis=0, concat_axis=0, tiled=True).reshape(
            places, width
        )

    flat_slot = expert_ids * capacity + slot_ids
    slot_row = flat_slot[None, :]
    slot_column = flat_slot[:, None]

    w_output_other = swapped(w_output)
    c_here = to_experts(place(slot_row, out_grad, places))
    o, q, k, v, p, ids = attend(
        hidden_in, gain1, w_query, w_key, w_value, bias_table, bucket_ids
    )
    o, w_output_other = lax.optimization_barrier((o, w_output_other))
    o_other = swapped(o)
    hmid, x_send = middle(
        mp[None], o, o_other, w_output, w_output_other, hidden_in, gain2, slot_row, places
    )
    x_here = to_experts(x_send)

    dx, hid, dpre, deo, gate, dlog = expert(x_here, c_here, w_in[0], w_out[0], router, dp[None])
    dx_home = to_experts(dx)
    eo = (gate * dot(hid, w_out[0])).astype(bf16)
    grad_w_out = contract_rows(hid, deo)[None]
    grad_w_in = contract_rows(x_here, dpre)[None]
    grad_router = contract_rows(dlog, x_here.astype(f32), lax.Precision.HIGHEST)
    dx_home, eo, grad_w_out, grad_w_in, grad_router = lax.optimization_barrier(
        (dx_home, eo, grad_w_out, grad_w_in, grad_router)
    )

    dn2 = pick(slot_column, dx_home)
    dn2_other = swapped(dn2)
    eo_home = to_experts(eo)
    dh, da, do, grad_norm2 = middle_back(dn2, dn2_other, hmid, out_grad, gain2, w_output)
    do, eo_home = lax.optimization_barrier((do, eo_home))
    dn1, keep_a, send_a, keep_b, send_b = attend_back(
        side, do, q, k, v, p, w_query, w_key, w_value, o, da, hidden_in, gain1, ids,
        grad_router, grad_norm2, bias_table,
    )
    dn1_other = swapped(dn1)

    order_a = tuple(range(1, bits))
    order_b = (2, 1) + tuple(range(3, bits))
    a = add(keep_a, exchange(send_a, count, 0))
    b = add(keep_b, exchange(send_b, count, 0))
    picked = pick(slot_column, eo_home)
    for bit_a, bit_b in zip(order_a, order_b):
        keep_a, send_a = halves(a, bit_a)
        keep_b, send_b = halves(b, bit_b)
        got_a = exchange(send_a, count, bit_a)
        got_b = exchange(send_b, count, bit_b)
        a, b = add(keep_a, got_a), add(keep_b, got_b)
    a, b, picked, dn1_other = lax.optimization_barrier((a, b, picked, dn1_other))
    picked_other = swapped(picked)
    grad_hidden = input_back(dn1, dn1_other, hidden_in, dh, gain1)
    for bit_a, bit_b in zip(order_a[::-1], order_b[::-1]):
        got_a = exchange(a, count, bit_a)
        got_b = exchange(b, count, bit_b)
        a, b = join(a, got_a, bit_a), join(b, got_b, bit_b)
    local = a.shape[0]
    a_got = exchange(a, count, 0)
    b_got = exchange(b[:local], count, 0)
    small_got = swapped(b[local:])
    hidden_out = finish(picked, picked_other, hmid)
    hidden_out, grad_hidden, a_got, b_got, small_got = lax.optimization_barrier(
        (hidden_out, grad_hidden, a_got, b_got, small_got)
    )
    grad_q, grad_k, grad_v, grad_w_output, grad_router, grad_table, grad_norm1, grad_norm2 = unpack(
        side, a, a_got, b, b_got, small_got, experts, buckets, heads
    )
    return (
        hidden_out,
        grad_hidden,
        grad_norm1[0],
        grad_q,
        grad_k,
        grad_v,
        grad_w_output,
        grad_table,
        grad_norm2[0],
        grad_router,
        grad_w_in,
        grad_w_out,
    )


def solution(mesh):
    return jax.shard_map(
        functools.partial(shards, mesh.shape["dp"]),
        mesh=mesh,
        in_specs=(
            P("dp", None),
            P(),
            P(None, "mp"),
            P(None, "mp"),
            P(None, "mp"),
            P("mp", None),
            P(None, "mp"),
            P(),
            P(),
            P(),
            P("dp", None, "mp"),
            P("dp", "mp", None),
            P("dp"),
            P("dp"),
            P("dp", None),
        ),
        out_specs=(
            P("dp", None),
            P("dp", None),
            P(),
            P(None, "mp"),
            P(None, "mp"),
            P(None, "mp"),
            P("mp", None),
            P(None, "mp"),
            P(),
            P(),
            P("dp", None, "mp"),
            P("dp", "mp", None),
        ),
        check_vma=False,
    )
```

```python
import functools

import jax
import jax.numpy as jnp
from jax import lax
from jax.experimental import pallas as pl
from jax.experimental.pallas import tpu as pltpu
from jax.sharding import PartitionSpec as P

epsilon = 1e-06
bf16 = jnp.bfloat16
f32 = jnp.float32
gelu_scale = 0.7978845608028654
gelu_cubic = 0.044715


def dot(left, right):
    return jnp.dot(left, right, preferred_element_type=f32)


def contract_last(left, right):
    return lax.dot_general(left, right, (((1,), (1,)), ((), ())), preferred_element_type=f32)


def contract_rows(left, right, precision=None):
    return lax.dot_general(
        left, right, (((0,), (0,)), ((), ())), preferred_element_type=f32, precision=precision
    )


def whole(shape):
    return pl.BlockSpec(shape, lambda *_: (0,) * len(shape))


def scalars():
    return pl.BlockSpec(memory_space=pltpu.SMEM)


def params(mib=62):
    return pltpu.CompilerParams(vmem_limit_bytes=mib * 1024 * 1024)


def cost(flops, moved):
    return pl.CostEstimate(flops=flops, bytes_accessed=moved, transcendentals=0)


def attend_kernel(
    x_ref, gain_ref, wq_ref, wk_ref, wv_ref, table_ref, first_ref, last_ref,
    o_ref, q_ref, k_ref, v_ref, p_ref, ids_ref, n_ref, bias_ref,
):
    pair = pl.program_id(0)
    length = x_ref.shape[0]
    buckets = table_ref.shape[1]
    half = o_ref.shape[1] // 2
    scale = half ** (-0.5)
    blocks = length // 128

    @pl.when(pair == 0)
    def _():
        x = x_ref[...].astype(f32)
        inverse = lax.rsqrt(jnp.mean(x * x, axis=-1, keepdims=True) + epsilon)
        n_ref[...] = (x * inverse * gain_ref[...][None, :]).astype(bf16)
        blank = jnp.zeros((8, length), jnp.int32)
        ahead = jnp.concatenate([jnp.broadcast_to(first_ref[0:1, :], (8, length)), blank], axis=1)
        behind = jnp.concatenate([jnp.broadcast_to(last_ref[7:8, :], (8, length)), blank], axis=1)
        place = lax.broadcasted_iota(jnp.int32, (8, 2 * length), 1)
        row = lax.broadcasted_iota(jnp.int32, (8, 2 * length), 0)
        line = jnp.where(place < length, behind, pltpu.roll(ahead, length - 1, 1))
        ids = line
        for r in range(1, 8):
            ids = jnp.where(row == r, pltpu.roll(line, r, 1), ids)
        ids_ref[...] = ids

    normed = n_ref[...]
    q = dot(normed, wq_ref[...]).astype(bf16)
    k = dot(normed, wk_ref[...]).astype(bf16)
    v = dot(normed, wv_ref[...]).astype(bf16)
    q_ref[...] = q
    k_ref[...] = k
    v_ref[...] = v
    ids = ids_ref[...]
    lane = lax.broadcasted_iota(jnp.int32, (length, 2 * half), 1)
    zero = jnp.zeros_like(q)
    out = None
    for h in range(2):
        head = 2 * pair + h
        mine = (lane < half) if h == 0 else (lane >= half)
        spread = jnp.zeros(ids.shape, f32)
        for b in range(buckets):
            spread = jnp.where(ids == b, table_ref[head, b], spread)
        for a in range(16):
            left = 127 - 8 * a
            bias_ref[8 * a : 8 * a + 8, :] = pltpu.roll(spread, 2 * length - left, 1)
        q_head = jnp.where(mine, q, zero)
        for i in range(blocks):
            rows = slice(128 * i, 128 * i + 128)
            start = 128 * (blocks - 1 - i)
            s = contract_last(q_head[rows], k) * scale + bias_ref[:, start : start + length]
            e = jnp.exp(s - jnp.max(s, axis=-1, keepdims=True))
            p = e * (1.0 / jnp.sum(e, axis=-1, keepdims=True))
            p_ref[h, rows, :] = p.astype(bf16)
        part = dot(p_ref[h], jnp.where(mine, v, zero))
        out = part if out is None else out + part
    o_ref[...] = out.astype(bf16)


def attend(x, gain, wq, wk, wv, table, bucket_ids):
    length, width = x.shape
    local = wq.shape[1]
    heads = table.shape[0]
    span = 2 * local // heads
    column = pl.BlockSpec((length, span), lambda j: (0, j))
    weight = pl.BlockSpec((width, span), lambda j: (0, j))
    thin = jax.ShapeDtypeStruct((length, local), bf16)
    return pl.pallas_call(
        attend_kernel,
        grid=(heads // 2,),
        in_specs=[
            whole((length, width)), whole((width,)), weight, weight, weight, scalars(),
            pl.BlockSpec((8, length), lambda j: (0, 0)),
            pl.BlockSpec((8, length), lambda j: (length // 8 - 1, 0)),
        ],
        out_specs=[
            column, column, column, column,
            pl.BlockSpec((2, length, length), lambda j: (j, 0, 0)),
            whole((8, 2 * length)),
        ],
        out_shape=[
            thin, thin, thin, thin,
            jax.ShapeDtypeStruct((heads, length, length), bf16),
            jax.ShapeDtypeStruct((8, 2 * length), jnp.int32),
        ],
        scratch_shapes=[pltpu.VMEM((length, width), bf16), pltpu.VMEM((128, 2 * length), f32)],
        compiler_params=params(),
        cost_estimate=cost(9_000_000_000, 9_000_000),
        name="attend",
    )(x, gain, wq, wk, wv, table, bucket_ids, bucket_ids)


def attend_back_kernel(
    buckets, side_ref, do_ref, q_ref, k_ref, v_ref, p_ref, wq_ref, wk_ref, wv_ref,
    o_ref, da_ref, x_ref, gain_ref, ids_ref, router_ref, norm2_ref,
    dn_ref, keep_ref, send_ref,
    ds_ref, acc_ref, total_ref, n_ref, small_ref,
):
    pair = pl.program_id(0)
    last = pl.num_programs(0) - 1
    length = do_ref.shape[0]
    span = do_ref.shape[1]
    half = span // 2
    scale = half ** (-0.5)
    blocks = length // 128
    experts = router_ref.shape[0]
    extra = small_ref.shape[0]
    local = keep_ref.shape[0] // 2 - extra
    quarter = local // 2
    even = side_ref[0] == 0

    @pl.when(pair == 0)
    def _():
        x = x_ref[...].astype(f32)
        inverse = lax.rsqrt(jnp.mean(x * x, axis=-1, keepdims=True) + epsilon)
        n_ref[...] = (x * inverse * gain_ref[...][None, :]).astype(bf16)
        small_ref[...] = jnp.zeros_like(small_ref)
        small_ref[0:experts, :] = router_ref[...]
        small_ref[experts + 1 : experts + 2, :] = norm2_ref[...]

    do = do_ref[...]
    q = q_ref[...]
    k = k_ref[...]
    v = v_ref[...]
    ids = ids_ref[...]
    q_turned = q.T
    do_turned = do.T
    lane = lax.broadcasted_iota(jnp.int32, (length, span), 1)
    zero = jnp.zeros_like(q)
    dq = None
    dk_parts = []
    dv_parts = []
    for h in range(2):
        mine = (lane < half) if h == 0 else (lane >= half)
        do_head = jnp.where(mine, do, zero)
        acc_ref[...] = jnp.zeros_like(acc_ref)
        for i in range(blocks):
            rows = slice(128 * i, 128 * i + 128)
            start = 128 * (blocks - 1 - i)
            p = p_ref[h, rows, :].astype(f32)
            dp = contract_last(do_head[rows], v)
            ds = p * (dp - jnp.sum(p * dp, axis=-1, keepdims=True))
            acc_ref[:, start : start + length] += ds
            ds_ref[rows, :] = ds.astype(bf16)
        ds_all = ds_ref[...]
        part = dot(ds_all, jnp.where(mine, k, zero))
        dq = part if dq is None else dq + part
        dk_parts.append(dot(q_turned[h * half : (h + 1) * half], ds_all))
        dv_parts.append(dot(do_turned[h * half : (h + 1) * half], p_ref[h]))
        diag = None
        for a in range(16):
            piece = pltpu.roll(acc_ref[8 * a : 8 * a + 8, :], 127 - 8 * a, 1)
            diag = piece if diag is None else diag + piece
        lines = []
        for b in range(buckets):
            hit = jnp.where(ids == b, diag, 0.0)
            fold = hit[:, 0:128]
            for y in range(1, 2 * length // 128):
                fold = fold + hit[:, 128 * y : 128 * y + 128]
            lines.append(jnp.sum(fold, axis=0, keepdims=True))
        lines.append(jnp.zeros((128 - buckets, 128), f32))
        sums = jnp.sum(jnp.concatenate(lines, axis=0).T, axis=0, keepdims=True)
        row = lax.broadcasted_iota(jnp.int32, (small_ref.shape[0], 128), 0)
        small_ref[:, 0:128] = jnp.where(
            row == experts + 2 + 2 * pair + h, sums, small_ref[:, 0:128]
        )
    dq_low = (dq * scale).astype(bf16)
    dk_turned = (jnp.concatenate(dk_parts, axis=0) * scale).astype(bf16)
    dv_turned = jnp.concatenate(dv_parts, axis=0).astype(bf16)
    part = (
        contract_last(dq_low, wq_ref[...])
        + contract_last(dk_turned.T, wk_ref[...])
        + contract_last(dv_turned.T, wv_ref[...])
    )
    normed = n_ref[...]
    here = pl.ds(pl.multiple_of(pair * span, span), span)
    grad_k = dot(dk_turned, normed).astype(bf16)
    grad_v = dot(dv_turned, normed).astype(bf16)
    keep_ref[here, :] = jnp.where(even, grad_k, grad_v)
    send_ref[here, :] = jnp.where(even, grad_v, grad_k)
    grad_q = dot(dq_low.T, normed).astype(bf16)
    grad_o = dot(o_ref[...].T, da_ref[...]).astype(bf16)
    keep = jnp.where(even, grad_q, grad_o)
    send = jnp.where(even, grad_o, grad_q)
    for i in range(0, span, 64):
        row = pair * span + i
        skip = jnp.where(row >= quarter, extra, 0)
        after = pl.ds(pl.multiple_of(local + row + skip, 64), 64)
        keep_ref[after, :] = keep[i : i + 64]
        send_ref[after, :] = send[i : i + 64]

    @pl.when(pair == 0)
    def _():
        total_ref[...] = part

    @pl.when(pair > 0)
    def _():
        total_ref[...] += part

    @pl.when(pair == last)
    def _():
        total = total_ref[...]
        dn_ref[...] = total.astype(bf16)
        x = x_ref[...].astype(f32)
        inverse = lax.rsqrt(jnp.mean(x * x, axis=-1, keepdims=True) + epsilon)
        small_ref[experts : experts + 1, :] = jnp.sum(
            total * x * inverse, axis=0, keepdims=True
        )
        small = small_ref[...].astype(bf16)
        for start in (local + quarter, 2 * local + extra):
            keep_ref[start : start + extra, :] = small
            send_ref[start : start + extra, :] = small


def small_rows(experts, heads):
    return -(-(experts + 2 + heads) // 64) * 64


def attend_back(side, do, q, k, v, p, wq, wk, wv, o, da, x, gain, ids, router, norm2, buckets):
    length, local = do.shape
    width = wq.shape[0]
    heads = p.shape[0]
    experts = router.shape[0]
    span = 2 * local // heads
    extra = small_rows(experts, heads)
    column = pl.BlockSpec((length, span), lambda j: (0, j))
    weight = pl.BlockSpec((width, span), lambda j: (0, j))
    part = jax.ShapeDtypeStruct((2 * (local + extra), width), bf16)
    return pl.pallas_call(
        functools.partial(attend_back_kernel, buckets),
        grid=(heads // 2,),
        in_specs=[
            scalars(), column, column, column, column,
            pl.BlockSpec((2, length, length), lambda j: (j, 0, 0)),
            weight, weight, weight, column,
            whole((length, width)), whole((length, width)), whole((width,)),
            whole(ids.shape), whole((experts, width)), whole((1, width)),
        ],
        out_specs=[
            whole((length, width)), whole(part.shape), whole(part.shape),
        ],
        out_shape=[
            jax.ShapeDtypeStruct((length, width), bf16), part, part,
        ],
        scratch_shapes=[
            pltpu.VMEM((length, length), bf16),
            pltpu.VMEM((128, 2 * length), f32),
            pltpu.VMEM((length, width), f32),
            pltpu.VMEM((length, width), bf16),
            pltpu.VMEM((extra, width), f32),
        ],
        compiler_params=params(),
        cost_estimate=cost(12_000_000_000, 9_000_000),
        name="attend_back",
    )(side, do, q, k, v, p, wq, wk, wv, o, da, x, gain, ids, router, norm2)


def hits(ids, count, axis):
    shape = (count, ids.shape[1]) if axis == 0 else (ids.shape[0], count)
    return jnp.where(lax.broadcasted_iota(jnp.int32, shape, axis) == ids, 1.0, 0.0).astype(bf16)


def row_block(block, width, first=0):
    return pl.BlockSpec((block, width), lambda i: (first + i, 0))


def row_block(block, width, first=0):
    return pl.BlockSpec((block, width), lambda i: (first + i, 0))


def place_kernel(capacity, expert_ref, slot_ref, rows_ref, out_ref):
    ids = expert_ref[...] * capacity + slot_ref[...]
    out_ref[...] = dot(hits(ids, out_ref.shape[0], 0), rows_ref[...]).astype(bf16)


def place(capacity, ids, rows, places):
    return pl.pallas_call(
        functools.partial(place_kernel, capacity),
        out_shape=jax.ShapeDtypeStruct((places, rows.shape[1]), bf16),
        compiler_params=params(),
        cost_estimate=cost(1_000_000_000, 3_000_000),
        name="place",
    )(*ids, rows)


def pick_kernel(ids_ref, slots_ref, *out_refs):
    first = 0
    for out_ref in out_refs:
        count = out_ref.shape[0]
        ids = ids_ref[first : first + count, :]
        out_ref[...] = dot(hits(ids, slots_ref.shape[0], 1), slots_ref[...]).astype(bf16)
        first += count


def pick(ids, slots, parts):
    part = jax.ShapeDtypeStruct((ids.shape[0] // parts, slots.shape[1]), bf16)
    return pl.pallas_call(
        pick_kernel,
        out_shape=[part] * parts,
        compiler_params=params(),
        cost_estimate=cost(1_000_000_000, 3_000_000),
        name="pick",
    )(ids, slots)


def middle_kernel(
    capacity, place_ref, o_ref, o_other_ref, w_ref, w_near_ref, w_far_ref, x_ref, gain_ref,
    expert_ref, slot_ref, hmid_ref, out_ref,
):
    low = place_ref[0] == 0
    even = place_ref[1] == 0
    o, o_other = o_ref[...], o_other_ref[...]
    w, near, far = w_ref[...], w_near_ref[...], w_far_ref[...]
    w_other = jnp.concatenate([jnp.where(even, near, far), jnp.where(even, far, near)], axis=0)
    heads = jnp.concatenate([jnp.where(low, o, o_other), jnp.where(low, o_other, o)], axis=1)
    weight = jnp.concatenate([jnp.where(low, w, w_other), jnp.where(low, w_other, w)], axis=0)
    hmid = x_ref[...].astype(f32) + dot(heads, weight)
    hmid_ref[...] = hmid
    inverse = lax.rsqrt(jnp.mean(hmid * hmid, axis=-1, keepdims=True) + epsilon)
    normed = (hmid * inverse * gain_ref[...][None, :]).astype(bf16)
    ids = expert_ref[...] * capacity + slot_ref[...]
    out_ref[...] = dot(hits(ids, out_ref.shape[0], 0), normed).astype(bf16)


def middle(capacity, where, o, o_other, w, w_near, w_far, x, gain, ids, places):
    return pl.pallas_call(
        functools.partial(middle_kernel, capacity),
        in_specs=[scalars()] + [pl.BlockSpec(memory_space=pltpu.VMEM)] * 9,
        out_shape=[
            jax.ShapeDtypeStruct(x.shape, f32),
            jax.ShapeDtypeStruct((places, x.shape[1]), bf16),
        ],
        compiler_params=params(),
        cost_estimate=cost(2_000_000_000, 6_000_000),
        name="middle",
    )(where, o, o_other, w, w_near, w_far, x, gain, *ids)


def middle_back_kernel(
    own_ref, got_ref, hmid_ref, c_ref, gain_ref, w_ref, *refs
):
    dh_ref, da_ref, do_ref, norm_ref = refs[-4:]
    hmid = hmid_ref[...]
    dn = own_ref[...].astype(f32) + got_ref[...].astype(f32)
    inverse = lax.rsqrt(jnp.mean(hmid * hmid, axis=-1, keepdims=True) + epsilon)
    scaled = dn * gain_ref[...][None, :]
    inner = jnp.mean(scaled * hmid, axis=-1, keepdims=True)
    dh = c_ref[...].astype(f32) + inverse * scaled - hmid * (inverse * inverse * inverse * inner)
    dh_ref[...] = dh
    da = dh.astype(bf16)
    da_ref[...] = da
    do_ref[...] = contract_last(da, w_ref[...]).astype(bf16)
    norm = jnp.sum(dn * hmid * inverse, axis=0, keepdims=True)
    before = refs[3][...] if len(refs) > 4 else jnp.zeros_like(norm)

    @pl.when(pl.program_id(0) == 0)
    def _():
        norm_ref[...] = before + norm

    @pl.when(pl.program_id(0) > 0)
    def _():
        norm_ref[...] += norm


def middle_back(first, own, got, hmid, c, gain, w, before=()):
    count, width = own.shape
    tokens = hmid.shape[0]
    local = w.shape[0]
    block = count
    here = first // block
    anywhere = pl.BlockSpec(memory_space=pl.ANY)
    return pl.pallas_call(
        middle_back_kernel,
        grid=(count // block,),
        in_specs=[
            row_block(block, width), row_block(block, width),
            row_block(block, width, here), row_block(block, width, here),
            whole(gain.shape), whole(w.shape),
        ] + ([anywhere] * 3 + [whole((1, width))] if before else []),
        out_specs=[
            row_block(block, width, here), row_block(block, width, here),
            row_block(block, local, here), whole((1, width)),
        ],
        out_shape=[
            jax.ShapeDtypeStruct((tokens, width), f32),
            jax.ShapeDtypeStruct((tokens, width), bf16),
            jax.ShapeDtypeStruct((tokens, local), bf16),
            jax.ShapeDtypeStruct((1, width), f32),
        ],
        input_output_aliases={6: 0, 7: 1, 8: 2} if before else {},
        compiler_params=params(),
        cost_estimate=cost(1_000_000_000, 6_000_000),
        name="middle_back",
    )(own, got, hmid, c, gain, w, *before)


def output_kernel(
    place_ref, own_ref, got_ref, x_ref, dh_ref, gain_ref, y_ref, y_other_ref, hmid_ref,
    grad_ref, out_ref,
):
    low = place_ref[0] == 0
    x = x_ref[...].astype(f32)
    dn = own_ref[...].astype(f32) + got_ref[...].astype(f32)
    inverse = lax.rsqrt(jnp.mean(x * x, axis=-1, keepdims=True) + epsilon)
    scaled = dn * gain_ref[...][None, :]
    inner = jnp.mean(scaled * x, axis=-1, keepdims=True)
    grad_ref[...] = dh_ref[...] + inverse * scaled - x * (inverse * inverse * inverse * inner)
    y, y_other = y_ref[...], y_other_ref[...]
    moved = jnp.concatenate([jnp.where(low, y, y_other), jnp.where(low, y_other, y)], axis=1)
    out_ref[...] = (hmid_ref[...] + moved.astype(f32)).astype(bf16)


def outputs(where, own, got, x, dh, gain, y, y_other, hmid):
    return pl.pallas_call(
        output_kernel,
        in_specs=[scalars()] + [pl.BlockSpec(memory_space=pltpu.VMEM)] * 8,
        out_shape=[
            jax.ShapeDtypeStruct(dh.shape, f32),
            jax.ShapeDtypeStruct(x.shape, bf16),
        ],
        compiler_params=params(),
        cost_estimate=cost(100_000_000, 10_000_000),
        name="outputs",
    )(where, own, got, x, dh, gain, y, y_other, hmid)


def split(value, low):
    n = value.shape[0] // 2
    first, second = value[:n], value[n:]
    return jnp.where(low, first, second), jnp.where(low, second, first)


def pair_up(value, got, low):
    return jnp.concatenate([jnp.where(low, value, got), jnp.where(low, got, value)], axis=0)


def unpack_kernel(
    experts, place_ref, a_ref, a_got_ref, b_ref, b_got_ref, small_ref, s_got_ref,
    q_ref, k_ref, v_ref, o_ref, router_ref, table_ref, norm1_ref, norm2_ref,
):
    even = place_ref[1] == 0
    heads, buckets = table_ref.shape
    a, a_got = a_ref[...], a_got_ref[...]
    b, b_got = b_ref[...], b_got_ref[...]
    k_ref[...] = jnp.where(even, a, a_got).T.astype(f32)
    v_ref[...] = jnp.where(even, a_got, a).T.astype(f32)
    q_ref[...] = jnp.where(even, b, b_got).T.astype(f32)
    o_ref[...] = jnp.where(even, b_got, b).astype(f32)
    small = small_ref[...].astype(f32)
    both = small + s_got_ref[...].astype(f32)
    router_ref[...] = both[:experts]
    norm1_ref[...] = both[experts]
    norm2_ref[...] = small[experts + 1]
    table_ref[...] = small[experts + 2 : experts + 2 + heads, :buckets]


def unpack(where, a, a_got, b, b_got, small, s_got, experts, buckets, heads):
    local, width = a.shape
    turned = jax.ShapeDtypeStruct((width, local), f32)
    flat = jax.ShapeDtypeStruct((width,), f32)
    return pl.pallas_call(
        functools.partial(unpack_kernel, experts),
        in_specs=[scalars()] + [pl.BlockSpec(memory_space=pltpu.VMEM)] * 6,
        out_shape=[
            turned, turned, turned,
            jax.ShapeDtypeStruct((local, width), f32),
            jax.ShapeDtypeStruct((experts, width), f32),
            jax.ShapeDtypeStruct((heads, buckets), f32),
            flat, flat,
        ],
        compiler_params=params(),
        cost_estimate=cost(100_000_000, 8_000_000),
        name="unpack",
    )(where, a, a_got, b, b_got, small, s_got)


def expert_kernel(
    x_ref, c_ref, w_in_ref, w_out_ref, router_ref, mine_ref,
    dx_ref, hid_ref, dpre_ref, deo_ref, gate_ref, dlog_ref,
    pre_ref, up_ref, probs_ref, inner_ref, total_ref,
):
    step = pl.program_id(0)
    rows = x_ref.shape[0]
    chunk = 64
    hot = lax.broadcasted_iota(jnp.int32, probs_ref.shape, 1) == mine_ref[0]

    @pl.when(step == 0)
    def _():
        router = router_ref[...]
        high = router.astype(bf16)
        rest = (router - high.astype(f32)).astype(bf16)
        logits = contract_last(x_ref[...], high) + contract_last(x_ref[...], rest)
        e = jnp.exp(logits - jnp.max(logits, axis=-1, keepdims=True))
        probs = e / jnp.sum(e, axis=-1, keepdims=True)
        gate = jnp.sum(jnp.where(hot, probs, 0.0), axis=-1, keepdims=True)
        probs_ref[...] = probs
        gate_ref[...] = gate
        deo_ref[...] = (gate * c_ref[...].astype(f32)).astype(bf16)

    pre_ref[...] = dot(x_ref[...], w_in_ref[...])
    up_ref[...] = contract_last(deo_ref[...], w_out_ref[...])
    for r in range(0, rows, chunk):
        part = slice(r, r + chunk)
        u = pre_ref[part, :]
        up = up_ref[part, :]
        square = u * u
        t = jnp.tanh(gelu_scale * u * (1.0 + gelu_cubic * square))
        side = 0.5 * (1.0 + t)
        hid = u * side
        slope = side + (0.5 * gelu_scale) * u * (1.0 - t * t) * (1.0 + (3.0 * gelu_cubic) * square)
        hid_ref[part, :] = hid.astype(bf16)
        dpre_ref[part, :] = (up * slope).astype(bf16)
        inner = jnp.sum(hid * up, axis=-1, keepdims=True)
        before = jnp.where(step == 0, 0.0, inner_ref[part, :])
        inner_ref[part, :] = before + inner
    part = contract_last(dpre_ref[...], w_in_ref[...])

    @pl.when(step == 0)
    def _():
        total_ref[...] = part

    @pl.when(step > 0)
    def _():
        total_ref[...] += part

    @pl.when(step == pl.num_programs(0) - 1)
    def _():
        dlog = inner_ref[...] * (hot.astype(f32) - probs_ref[...])
        dlog_ref[...] = dlog
        dx_ref[...] = (
            total_ref[...] + dot(dlog.astype(bf16), router_ref[...].astype(bf16))
        ).astype(bf16)


def expert(x, c, w_in, w_out, router, mine):
    rows, width = x.shape
    hidden = w_in.shape[1]
    experts = router.shape[0]
    step = 512 if hidden % 512 == 0 else hidden
    return pl.pallas_call(
        expert_kernel,
        grid=(hidden // step,),
        in_specs=[
            whole((rows, width)), whole((rows, width)),
            pl.BlockSpec((width, step), lambda j: (0, j)),
            pl.BlockSpec((step, width), lambda j: (j, 0)),
            whole((experts, width)), scalars(),
        ],
        out_specs=[
            whole((rows, width)),
            pl.BlockSpec((rows, step), lambda j: (0, j)),
            pl.BlockSpec((rows, step), lambda j: (0, j)),
            whole((rows, width)), whole((rows, 1)), whole((rows, experts)),
        ],
        out_shape=[
            jax.ShapeDtypeStruct((rows, width), bf16),
            jax.ShapeDtypeStruct((rows, hidden), bf16),
            jax.ShapeDtypeStruct((rows, hidden), bf16),
            jax.ShapeDtypeStruct((rows, width), bf16),
            jax.ShapeDtypeStruct((rows, 1), f32),
            jax.ShapeDtypeStruct((rows, experts), f32),
        ],
        scratch_shapes=[
            pltpu.VMEM((rows, step), f32),
            pltpu.VMEM((rows, step), f32),
            pltpu.VMEM((rows, experts), f32),
            pltpu.VMEM((rows, 1), f32),
            pltpu.VMEM((rows, width), f32),
        ],
        compiler_params=params(),
        cost_estimate=cost(4_500_000_000, 12_000_000),
        name="expert",
    )(x, c, w_in, w_out, router, mine)


def exchange(value, count, bit):
    return lax.ppermute(value, "dp", [(i, i ^ (1 << bit)) for i in range(count)])


def add(left, right):
    return (left.astype(f32) + right.astype(f32)).astype(left.dtype)


def shards(
    count,
    hidden_in,
    norm1_gain,
    w_query,
    w_key,
    w_value,
    w_output,
    bias_table,
    bucket_ids,
    norm2_gain,
    router,
    w_in,
    w_out,
    expert_ids,
    slot_ids,
    out_grad,
):
    tokens, width = hidden_in.shape
    buckets, heads = bias_table.shape
    experts = router.shape[1]
    capacity = max(2, 5 * tokens // (4 * experts))
    places = experts * capacity
    bits = (count - 1).bit_length()
    swap = [(0, 1), (1, 0)]
    mp = lax.axis_index("mp").astype(jnp.int32)
    dp = lax.axis_index("dp").astype(jnp.int32)
    side = (dp & 1)[None]
    where = jnp.stack([mp] + [(dp >> bit) & 1 for bit in range(bits)])

    def swapped(value):
        return lax.ppermute(value, "mp", swap)

    def to_experts(rows):
        block = rows.reshape(experts, capacity, -1)
        return lax.all_to_all(block, "dp", split_axis=0, concat_axis=0, tiled=True).reshape(
            places, -1
        )

    slot_row = (expert_ids[None, :], slot_ids[None, :])
    slot_column = (expert_ids * capacity + slot_ids)[:, None]

    w_near, _ = split(w_output, (dp & 1) == 0)
    w_near = swapped(w_near)
    c_here = to_experts(place(capacity, slot_row, out_grad, places))
    o, q, k, v, p, ids = attend(
        hidden_in, norm1_gain, w_query, w_key, w_value, bias_table.T, bucket_ids
    )
    o, w_near = lax.optimization_barrier((o, w_near))
    o_other = swapped(o)
    w_far = exchange(w_near, count, 0)
    hmid, x_send = middle(
        capacity, where, o, o_other, w_output, w_near, w_far, hidden_in, norm2_gain, slot_row, places
    )
    x_here = to_experts(x_send)

    dx, hid, dpre, deo, gate, dlog = expert(x_here, c_here, w_in[0], w_out[0], router.T, dp[None])
    dx_home = to_experts(dx)
    eo = (gate * dot(hid, w_out[0])).astype(bf16)
    eo_mine = jnp.where(mp == 0, eo[:, : width // 2], eo[:, width // 2 :])
    eo_other = swapped(jnp.where(mp == 0, eo[:, width // 2 :], eo[:, : width // 2]))
    grad_w_out = contract_rows(hid, deo)[None]
    grad_w_in = contract_rows(x_here, dpre)[None]
    grad_router = contract_rows(dlog, x_here.astype(f32), lax.Precision.HIGHEST)
    eo = add(eo_mine, eo_other)
    dx_home, grad_w_out, grad_w_in, grad_router = lax.optimization_barrier(
        (dx_home, grad_w_out, grad_w_in, grad_router)
    )

    low, high = pick(slot_column, dx_home, 2)
    low, high, eo = lax.optimization_barrier((low, high, eo))
    low_other = swapped(low)
    high_other = swapped(high)
    eo_home = to_experts(eo)
    before = middle_back(0, low, low_other, hmid, out_grad, norm2_gain, w_output)
    dh, da, do, grad_norm2 = middle_back(
        tokens // 2, high, high_other, hmid, out_grad, norm2_gain, w_output, before
    )
    dn1, keep, send = attend_back(
        side, do, q, k, v, p, w_query, w_key, w_value, o, da, hidden_in, norm1_gain, ids,
        grad_router, grad_norm2, buckets,
    )
    dn1, keep, send, eo_home = lax.optimization_barrier((dn1, keep, send, eo_home))
    dn1_other = swapped(dn1)

    local = q.shape[1]
    order_a = tuple(range(1, bits))
    order_b = (2, 1) + tuple(range(3, bits))
    total = add(keep, exchange(send, count, 0))
    a, b = total[:local], total[local:]
    for stage, (bit_a, bit_b) in enumerate(zip(order_a[:-1], order_b[:-1])):
        keep_a, send_a = split(a, where[bit_a + 1] == 0)
        keep_b, send_b = split(b, where[bit_b + 1] == 0)
        got_a = exchange(send_a, count, bit_a)
        got_b = exchange(send_b, count, bit_b)
        if stage == 0:
            (picked,) = pick(slot_column, eo_home, 1)
            got_a, got_b, picked = lax.optimization_barrier((got_a, got_b, picked))
        a, b = add(keep_a, got_a), add(keep_b, got_b)
    got_a = exchange(a, count, order_a[-1])
    got_b = exchange(b, count, order_b[-1])
    got_a, got_b, dn1_other = lax.optimization_barrier((got_a, got_b, dn1_other))
    picked_other = swapped(picked)
    a, b = add(a, got_a), add(b, got_b)
    for bit_a, bit_b in zip(order_a[-2::-1], order_b[-2::-1]):
        got_a = exchange(a, count, bit_a)
        got_b = exchange(b, count, bit_b)
        if bit_b == 1:
            grad_hidden, hidden_out = outputs(
                where, dn1, dn1_other, hidden_in, dh, norm1_gain, picked, picked_other, hmid
            )
            got_a, got_b, grad_hidden, hidden_out = lax.optimization_barrier(
                (got_a, got_b, grad_hidden, hidden_out)
            )
        a = pair_up(a, got_a, where[bit_a + 1] == 0)
        b = pair_up(b, got_b, where[bit_b + 1] == 0)
        if bit_b == 1:
            small = b[local // 2 :]
            b = b[: local // 2]
            small_other = swapped(small)
    a, b, small_other = lax.optimization_barrier((a, b, small_other))
    grad_q, grad_k, grad_v, grad_w_output, grad_router, grad_table, grad_norm1, grad_norm2 = unpack(
        where, a, exchange(a, count, 0), b, exchange(b, count, 0), small, small_other,
        experts, buckets, heads,
    )
    return (
        hidden_out,
        grad_hidden,
        grad_norm1,
        grad_q,
        grad_k,
        grad_v,
        grad_w_output,
        grad_table.T,
        grad_norm2,
        grad_router.T,
        grad_w_in,
        grad_w_out,
    )


def solution(mesh):
    return jax.shard_map(
        functools.partial(shards, mesh.shape["dp"]),
        mesh=mesh,
        in_specs=(
            P("dp", None),
            P(),
            P(None, "mp"),
            P(None, "mp"),
            P(None, "mp"),
            P("mp", None),
            P(None, "mp"),
            P(),
            P(),
            P(),
            P("dp", None, "mp"),
            P("dp", "mp", None),
            P("dp"),
            P("dp"),
            P("dp", None),
        ),
        out_specs=(
            P("dp", None),
            P("dp", None),
            P(),
            P(None, "mp"),
            P(None, "mp"),
            P(None, "mp"),
            P("mp", None),
            P(None, "mp"),
            P(),
            P(),
            P("dp", None, "mp"),
            P("dp", "mp", None),
        ),
        check_vma=False,
    )
```

```python
import functools

import jax
import jax.numpy as jnp
from jax import lax
from jax.experimental import pallas as pl
from jax.experimental.pallas import tpu as pltpu
from jax.sharding import PartitionSpec as P

epsilon = 1e-06
bf16 = jnp.bfloat16
f32 = jnp.float32
gelu_scale = 0.7978845608028654
gelu_cubic = 0.044715


def dot(left, right):
    return jnp.dot(left, right, preferred_element_type=f32)


def contract_last(left, right):
    return lax.dot_general(left, right, (((1,), (1,)), ((), ())), preferred_element_type=f32)


def contract_rows(left, right, precision=None):
    return lax.dot_general(
        left, right, (((0,), (0,)), ((), ())), preferred_element_type=f32, precision=precision
    )


def whole(shape):
    return pl.BlockSpec(shape, lambda *_: (0,) * len(shape))


def scalars():
    return pl.BlockSpec(memory_space=pltpu.SMEM)


def params(mib=62):
    return pltpu.CompilerParams(vmem_limit_bytes=mib * 1024 * 1024)


def cost(flops, moved):
    return pl.CostEstimate(flops=flops, bytes_accessed=moved, transcendentals=0)


def attend_kernel(
    x_ref, gain_ref, wq_ref, wk_ref, wv_ref, table_ref, first_ref, last_ref,
    o_ref, q_ref, k_ref, v_ref, p_ref, ids_ref, n_ref, bias_ref,
):
    pair = pl.program_id(0)
    length = x_ref.shape[0]
    buckets = table_ref.shape[1]
    half = o_ref.shape[1] // 2
    scale = half ** (-0.5)
    blocks = length // 128

    @pl.when(pair == 0)
    def _():
        x = x_ref[...].astype(f32)
        inverse = lax.rsqrt(jnp.mean(x * x, axis=-1, keepdims=True) + epsilon)
        n_ref[...] = (x * inverse * gain_ref[...][None, :]).astype(bf16)
        blank = jnp.zeros((8, length), jnp.int32)
        ahead = jnp.concatenate([jnp.broadcast_to(first_ref[0:1, :], (8, length)), blank], axis=1)
        behind = jnp.concatenate([jnp.broadcast_to(last_ref[7:8, :], (8, length)), blank], axis=1)
        place = lax.broadcasted_iota(jnp.int32, (8, 2 * length), 1)
        row = lax.broadcasted_iota(jnp.int32, (8, 2 * length), 0)
        line = jnp.where(place < length, behind, pltpu.roll(ahead, length - 1, 1))
        ids = line
        for r in range(1, 8):
            ids = jnp.where(row == r, pltpu.roll(line, r, 1), ids)
        ids_ref[...] = ids

    normed = n_ref[...]
    q = dot(normed, wq_ref[...]).astype(bf16)
    k = dot(normed, wk_ref[...]).astype(bf16)
    v = dot(normed, wv_ref[...]).astype(bf16)
    q_ref[...] = q
    k_ref[...] = k
    v_ref[...] = v
    ids = ids_ref[...]
    lane = lax.broadcasted_iota(jnp.int32, (length, 2 * half), 1)
    zero = jnp.zeros_like(q)
    out = None
    for h in range(2):
        head = 2 * pair + h
        mine = (lane < half) if h == 0 else (lane >= half)
        spread = jnp.zeros(ids.shape, f32)
        for b in range(buckets):
            spread = jnp.where(ids == b, table_ref[head, b], spread)
        for a in range(16):
            left = 127 - 8 * a
            bias_ref[8 * a : 8 * a + 8, :] = pltpu.roll(spread, 2 * length - left, 1)
        q_head = jnp.where(mine, q, zero)
        for i in range(blocks):
            rows = slice(128 * i, 128 * i + 128)
            start = 128 * (blocks - 1 - i)
            s = contract_last(q_head[rows], k) * scale + bias_ref[:, start : start + length]
            e = jnp.exp(s - jnp.max(s, axis=-1, keepdims=True))
            p = e * (1.0 / jnp.sum(e, axis=-1, keepdims=True))
            p_ref[h, rows, :] = p.astype(bf16)
        part = dot(p_ref[h], jnp.where(mine, v, zero))
        out = part if out is None else out + part
    o_ref[...] = out.astype(bf16)


def attend(x, gain, wq, wk, wv, table, bucket_ids):
    length, width = x.shape
    local = wq.shape[1]
    heads = table.shape[0]
    span = 2 * local // heads
    column = pl.BlockSpec((length, span), lambda j: (0, j))
    weight = pl.BlockSpec((width, span), lambda j: (0, j))
    thin = jax.ShapeDtypeStruct((length, local), bf16)
    return pl.pallas_call(
        attend_kernel,
        grid=(heads // 2,),
        in_specs=[
            whole((length, width)), whole((width,)), weight, weight, weight, scalars(),
            pl.BlockSpec((8, length), lambda j: (0, 0)),
            pl.BlockSpec((8, length), lambda j: (length // 8 - 1, 0)),
        ],
        out_specs=[
            column, column, column, column,
            pl.BlockSpec((2, length, length), lambda j: (j, 0, 0)),
            whole((8, 2 * length)),
        ],
        out_shape=[
            thin, thin, thin, thin,
            jax.ShapeDtypeStruct((heads, length, length), bf16),
            jax.ShapeDtypeStruct((8, 2 * length), jnp.int32),
        ],
        scratch_shapes=[pltpu.VMEM((length, width), bf16), pltpu.VMEM((128, 2 * length), f32)],
        compiler_params=params(),
        cost_estimate=cost(9_000_000_000, 9_000_000),
        name="attend",
    )(x, gain, wq, wk, wv, table, bucket_ids, bucket_ids)


def attend_back_kernel(
    buckets, side_ref, do_ref, q_ref, k_ref, v_ref, p_ref, wq_ref, wk_ref, wv_ref,
    o_ref, da_ref, x_ref, gain_ref, ids_ref, router_ref, norm2_ref,
    dn_ref, keep_ref, send_ref,
    ds_ref, acc_ref, total_ref, n_ref, small_ref,
):
    pair = pl.program_id(0)
    last = pl.num_programs(0) - 1
    length = do_ref.shape[0]
    span = do_ref.shape[1]
    half = span // 2
    scale = half ** (-0.5)
    blocks = length // 128
    experts = router_ref.shape[0]
    extra = small_ref.shape[0]
    local = keep_ref.shape[0] // 2 - extra
    quarter = local // 2
    even = side_ref[0] == 0

    @pl.when(pair == 0)
    def _():
        x = x_ref[...].astype(f32)
        inverse = lax.rsqrt(jnp.mean(x * x, axis=-1, keepdims=True) + epsilon)
        n_ref[...] = (x * inverse * gain_ref[...][None, :]).astype(bf16)
        small_ref[...] = jnp.zeros_like(small_ref)
        small_ref[0:experts, :] = router_ref[...]
        small_ref[experts + 1 : experts + 2, :] = norm2_ref[...]

    do = do_ref[...]
    q = q_ref[...]
    k = k_ref[...]
    v = v_ref[...]
    ids = ids_ref[...]
    q_turned = q.T
    do_turned = do.T
    lane = lax.broadcasted_iota(jnp.int32, (length, span), 1)
    zero = jnp.zeros_like(q)
    dq = None
    dk_parts = []
    dv_parts = []
    for h in range(2):
        mine = (lane < half) if h == 0 else (lane >= half)
        do_head = jnp.where(mine, do, zero)
        acc_ref[...] = jnp.zeros_like(acc_ref)
        for i in range(blocks):
            rows = slice(128 * i, 128 * i + 128)
            start = 128 * (blocks - 1 - i)
            p = p_ref[h, rows, :].astype(f32)
            dp = contract_last(do_head[rows], v)
            ds = p * (dp - jnp.sum(p * dp, axis=-1, keepdims=True))
            acc_ref[:, start : start + length] += ds
            ds_ref[rows, :] = ds.astype(bf16)
        ds_all = ds_ref[...]
        part = dot(ds_all, jnp.where(mine, k, zero))
        dq = part if dq is None else dq + part
        dk_parts.append(dot(q_turned[h * half : (h + 1) * half], ds_all))
        dv_parts.append(dot(do_turned[h * half : (h + 1) * half], p_ref[h]))
        diag = None
        for a in range(16):
            piece = pltpu.roll(acc_ref[8 * a : 8 * a + 8, :], 127 - 8 * a, 1)
            diag = piece if diag is None else diag + piece
        lines = []
        for b in range(buckets):
            hit = jnp.where(ids == b, diag, 0.0)
            fold = hit[:, 0:128]
            for y in range(1, 2 * length // 128):
                fold = fold + hit[:, 128 * y : 128 * y + 128]
            lines.append(jnp.sum(fold, axis=0, keepdims=True))
        lines.append(jnp.zeros((128 - buckets, 128), f32))
        sums = jnp.sum(jnp.concatenate(lines, axis=0).T, axis=0, keepdims=True)
        row = lax.broadcasted_iota(jnp.int32, (small_ref.shape[0], 128), 0)
        small_ref[:, 0:128] = jnp.where(
            row == experts + 2 + 2 * pair + h, sums, small_ref[:, 0:128]
        )
    dq_low = (dq * scale).astype(bf16)
    dk_turned = (jnp.concatenate(dk_parts, axis=0) * scale).astype(bf16)
    dv_turned = jnp.concatenate(dv_parts, axis=0).astype(bf16)
    part = (
        contract_last(dq_low, wq_ref[...])
        + contract_last(dk_turned.T, wk_ref[...])
        + contract_last(dv_turned.T, wv_ref[...])
    )
    normed = n_ref[...]
    here = pl.ds(pl.multiple_of(pair * span, span), span)
    grad_k = dot(dk_turned, normed).astype(bf16)
    grad_v = dot(dv_turned, normed).astype(bf16)
    keep_ref[here, :] = jnp.where(even, grad_k, grad_v)
    send_ref[here, :] = jnp.where(even, grad_v, grad_k)
    grad_q = dot(dq_low.T, normed).astype(bf16)
    grad_o = dot(o_ref[...].T, da_ref[...]).astype(bf16)
    keep = jnp.where(even, grad_q, grad_o)
    send = jnp.where(even, grad_o, grad_q)
    for i in range(0, span, 64):
        row = pair * span + i
        skip = jnp.where(row >= quarter, extra, 0)
        after = pl.ds(pl.multiple_of(local + row + skip, 32), 64)
        keep_ref[after, :] = keep[i : i + 64]
        send_ref[after, :] = send[i : i + 64]

    @pl.when(pair == 0)
    def _():
        total_ref[...] = part

    @pl.when(pair > 0)
    def _():
        total_ref[...] += part

    @pl.when(pair == last)
    def _():
        total = total_ref[...]
        dn_ref[...] = total.astype(bf16)
        x = x_ref[...].astype(f32)
        inverse = lax.rsqrt(jnp.mean(x * x, axis=-1, keepdims=True) + epsilon)
        small_ref[experts : experts + 1, :] = jnp.sum(
            total * x * inverse, axis=0, keepdims=True
        )
        small = small_ref[...].astype(bf16)
        for start in (local + quarter, 2 * local + extra):
            keep_ref[start : start + extra, :] = small
            send_ref[start : start + extra, :] = small


def small_rows(experts, heads):
    return -(-(experts + 2 + heads) // 32) * 32


def attend_back(side, do, q, k, v, p, wq, wk, wv, o, da, x, gain, ids, router, norm2, buckets):
    length, local = do.shape
    width = wq.shape[0]
    heads = p.shape[0]
    experts = router.shape[0]
    span = 2 * local // heads
    extra = small_rows(experts, heads)
    column = pl.BlockSpec((length, span), lambda j: (0, j))
    weight = pl.BlockSpec((width, span), lambda j: (0, j))
    part = jax.ShapeDtypeStruct((2 * (local + extra), width), bf16)
    return pl.pallas_call(
        functools.partial(attend_back_kernel, buckets),
        grid=(heads // 2,),
        in_specs=[
            scalars(), column, column, column, column,
            pl.BlockSpec((2, length, length), lambda j: (j, 0, 0)),
            weight, weight, weight, column,
            whole((length, width)), whole((length, width)), whole((width,)),
            whole(ids.shape), whole((experts, width)), whole((1, width)),
        ],
        out_specs=[
            whole((length, width)), whole(part.shape), whole(part.shape),
        ],
        out_shape=[
            jax.ShapeDtypeStruct((length, width), bf16), part, part,
        ],
        scratch_shapes=[
            pltpu.VMEM((length, length), bf16),
            pltpu.VMEM((128, 2 * length), f32),
            pltpu.VMEM((length, width), f32),
            pltpu.VMEM((length, width), bf16),
            pltpu.VMEM((extra, width), f32),
        ],
        compiler_params=params(),
        cost_estimate=cost(12_000_000_000, 9_000_000),
        name="attend_back",
    )(side, do, q, k, v, p, wq, wk, wv, o, da, x, gain, ids, router, norm2)


def hits(ids, count, axis):
    shape = (count, ids.shape[1]) if axis == 0 else (ids.shape[0], count)
    return jnp.where(lax.broadcasted_iota(jnp.int32, shape, axis) == ids, 1.0, 0.0).astype(bf16)


def row_block(block, width, first=0):
    return pl.BlockSpec((block, width), lambda i: (first + i, 0))


def row_block(block, width, first=0):
    return pl.BlockSpec((block, width), lambda i: (first + i, 0))


def place_kernel(capacity, expert_ref, slot_ref, rows_ref, out_ref):
    ids = expert_ref[...] * capacity + slot_ref[...]
    out_ref[...] = dot(hits(ids, out_ref.shape[0], 0), rows_ref[...]).astype(bf16)


def place(capacity, ids, rows, places):
    return pl.pallas_call(
        functools.partial(place_kernel, capacity),
        out_shape=jax.ShapeDtypeStruct((places, rows.shape[1]), bf16),
        compiler_params=params(),
        cost_estimate=cost(1_000_000_000, 3_000_000),
        name="place",
    )(*ids, rows)


def pick_kernel(ids_ref, slots_ref, *out_refs):
    first = 0
    for out_ref in out_refs:
        count = out_ref.shape[0]
        ids = ids_ref[first : first + count, :]
        out_ref[...] = dot(hits(ids, slots_ref.shape[0], 1), slots_ref[...]).astype(bf16)
        first += count


def pick(ids, slots, parts):
    part = jax.ShapeDtypeStruct((ids.shape[0] // parts, slots.shape[1]), bf16)
    return pl.pallas_call(
        pick_kernel,
        out_shape=[part] * parts,
        compiler_params=params(58),
        cost_estimate=cost(1_000_000_000, 3_000_000),
        name="pick",
    )(ids, slots)


def middle_kernel(
    capacity, place_ref, o_ref, o_other_ref, w_ref, w_near_ref, w_far_ref, x_ref, gain_ref,
    expert_ref, slot_ref, hmid_ref, out_ref,
):
    low = place_ref[0] == 0
    even = place_ref[1] == 0
    o, o_other = o_ref[...], o_other_ref[...]
    w, near, far = w_ref[...], w_near_ref[...], w_far_ref[...]
    w_other = jnp.concatenate([jnp.where(even, near, far), jnp.where(even, far, near)], axis=0)
    heads = jnp.concatenate([jnp.where(low, o, o_other), jnp.where(low, o_other, o)], axis=1)
    weight = jnp.concatenate([jnp.where(low, w, w_other), jnp.where(low, w_other, w)], axis=0)
    hmid = x_ref[...].astype(f32) + dot(heads, weight)
    hmid_ref[...] = hmid
    inverse = lax.rsqrt(jnp.mean(hmid * hmid, axis=-1, keepdims=True) + epsilon)
    normed = (hmid * inverse * gain_ref[...][None, :]).astype(bf16)
    ids = expert_ref[...] * capacity + slot_ref[...]
    out_ref[...] = dot(hits(ids, out_ref.shape[0], 0), normed).astype(bf16)


def middle(capacity, where, o, o_other, w, w_near, w_far, x, gain, ids, places):
    return pl.pallas_call(
        functools.partial(middle_kernel, capacity),
        in_specs=[scalars()] + [pl.BlockSpec(memory_space=pltpu.VMEM)] * 9,
        out_shape=[
            jax.ShapeDtypeStruct(x.shape, f32),
            jax.ShapeDtypeStruct((places, x.shape[1]), bf16),
        ],
        compiler_params=params(58),
        cost_estimate=cost(2_000_000_000, 6_000_000),
        name="middle",
    )(where, o, o_other, w, w_near, w_far, x, gain, *ids)


def middle_back_kernel(
    own_ref, got_ref, hmid_ref, c_ref, gain_ref, w_ref, *refs
):
    dh_ref, da_ref, do_ref, norm_ref = refs[-4:]
    hmid = hmid_ref[...]
    dn = own_ref[...].astype(f32) + got_ref[...].astype(f32)
    inverse = lax.rsqrt(jnp.mean(hmid * hmid, axis=-1, keepdims=True) + epsilon)
    scaled = dn * gain_ref[...][None, :]
    inner = jnp.mean(scaled * hmid, axis=-1, keepdims=True)
    dh = c_ref[...].astype(f32) + inverse * scaled - hmid * (inverse * inverse * inverse * inner)
    dh_ref[...] = dh
    da = dh.astype(bf16)
    da_ref[...] = da
    do_ref[...] = contract_last(da, w_ref[...]).astype(bf16)
    norm = jnp.sum(dn * hmid * inverse, axis=0, keepdims=True)
    before = refs[3][...] if len(refs) > 4 else jnp.zeros_like(norm)

    @pl.when(pl.program_id(0) == 0)
    def _():
        norm_ref[...] = before + norm

    @pl.when(pl.program_id(0) > 0)
    def _():
        norm_ref[...] += norm


def middle_back(first, own, got, hmid, c, gain, w, before=()):
    count, width = own.shape
    tokens = hmid.shape[0]
    local = w.shape[0]
    block = count
    here = first // block
    anywhere = pl.BlockSpec(memory_space=pl.ANY)
    return pl.pallas_call(
        middle_back_kernel,
        grid=(count // block,),
        in_specs=[
            row_block(block, width), row_block(block, width),
            row_block(block, width, here), row_block(block, width, here),
            whole(gain.shape), whole(w.shape),
        ] + ([anywhere] * 3 + [whole((1, width))] if before else []),
        out_specs=[
            row_block(block, width, here), row_block(block, width, here),
            row_block(block, local, here), whole((1, width)),
        ],
        out_shape=[
            jax.ShapeDtypeStruct((tokens, width), f32),
            jax.ShapeDtypeStruct((tokens, width), bf16),
            jax.ShapeDtypeStruct((tokens, local), bf16),
            jax.ShapeDtypeStruct((1, width), f32),
        ],
        input_output_aliases={6: 0, 7: 1, 8: 2} if before else {},
        compiler_params=params(58),
        cost_estimate=cost(1_000_000_000, 6_000_000),
        name="middle_back",
    )(own, got, hmid, c, gain, w, *before)


def output_kernel(
    place_ref, own_ref, got_ref, x_ref, dh_ref, gain_ref, y_ref, y_other_ref, hmid_ref,
    grad_ref, out_ref,
):
    low = place_ref[0] == 0
    x = x_ref[...].astype(f32)
    dn = own_ref[...].astype(f32) + got_ref[...].astype(f32)
    inverse = lax.rsqrt(jnp.mean(x * x, axis=-1, keepdims=True) + epsilon)
    scaled = dn * gain_ref[...][None, :]
    inner = jnp.mean(scaled * x, axis=-1, keepdims=True)
    grad_ref[...] = dh_ref[...] + inverse * scaled - x * (inverse * inverse * inverse * inner)
    y, y_other = y_ref[...], y_other_ref[...]
    moved = jnp.concatenate([jnp.where(low, y, y_other), jnp.where(low, y_other, y)], axis=1)
    out_ref[...] = (hmid_ref[...] + moved.astype(f32)).astype(bf16)


def outputs(where, own, got, x, dh, gain, y, y_other, hmid):
    return pl.pallas_call(
        output_kernel,
        in_specs=[scalars()] + [pl.BlockSpec(memory_space=pltpu.VMEM)] * 8,
        out_shape=[
            jax.ShapeDtypeStruct(dh.shape, f32),
            jax.ShapeDtypeStruct(x.shape, bf16),
        ],
        compiler_params=params(58),
        cost_estimate=cost(100_000_000, 10_000_000),
        name="outputs",
    )(where, own, got, x, dh, gain, y, y_other, hmid)


def split(value, low):
    n = value.shape[0] // 2
    first, second = value[:n], value[n:]
    return jnp.where(low, first, second), jnp.where(low, second, first)


def split_sum(pair, low):
    (keep, send), (got_keep, got_send) = split(pair[0], low), split(pair[1], low)
    return add(keep, got_keep), add(send, got_send)


def pair_up(value, got, low):
    return jnp.concatenate([jnp.where(low, value, got), jnp.where(low, got, value)], axis=0)


def unpack_kernel(
    experts, place_ref, a_ref, a_got_ref, b_ref, b_got_ref, small_ref, s_got_ref,
    q_ref, k_ref, v_ref, o_ref, router_ref, table_ref, norm1_ref, norm2_ref,
):
    even = place_ref[1] == 0
    heads, buckets = table_ref.shape
    a, a_got = a_ref[...], a_got_ref[...]
    b, b_got = b_ref[...], b_got_ref[...]
    k_ref[...] = jnp.where(even, a, a_got).T.astype(f32)
    v_ref[...] = jnp.where(even, a_got, a).T.astype(f32)
    q_ref[...] = jnp.where(even, b, b_got).T.astype(f32)
    o_ref[...] = jnp.where(even, b_got, b).astype(f32)
    small = small_ref[...].astype(f32)
    both = small + s_got_ref[...].astype(f32)
    router_ref[...] = both[:experts]
    norm1_ref[...] = both[experts]
    norm2_ref[...] = small[experts + 1]
    table_ref[...] = small[experts + 2 : experts + 2 + heads, :buckets]


def unpack(where, a, a_got, b, b_got, small, s_got, experts, buckets, heads):
    local, width = a.shape
    turned = jax.ShapeDtypeStruct((width, local), f32)
    flat = jax.ShapeDtypeStruct((width,), f32)
    return pl.pallas_call(
        functools.partial(unpack_kernel, experts),
        in_specs=[scalars()] + [pl.BlockSpec(memory_space=pltpu.VMEM)] * 6,
        out_shape=[
            turned, turned, turned,
            jax.ShapeDtypeStruct((local, width), f32),
            jax.ShapeDtypeStruct((experts, width), f32),
            jax.ShapeDtypeStruct((heads, buckets), f32),
            flat, flat,
        ],
        compiler_params=params(58),
        cost_estimate=cost(100_000_000, 8_000_000),
        name="unpack",
    )(where, a, a_got, b, b_got, small, s_got)


def expert_kernel(
    x_ref, c_ref, w_in_ref, w_out_ref, router_ref, mine_ref,
    dx_ref, hid_ref, dpre_ref, deo_ref, gate_ref, dlog_ref,
    pre_ref, up_ref, probs_ref, inner_ref, total_ref,
):
    step = pl.program_id(0)
    rows = x_ref.shape[0]
    chunk = 64
    hot = lax.broadcasted_iota(jnp.int32, probs_ref.shape, 1) == mine_ref[0]

    @pl.when(step == 0)
    def _():
        router = router_ref[...]
        high = router.astype(bf16)
        rest = (router - high.astype(f32)).astype(bf16)
        logits = contract_last(x_ref[...], high) + contract_last(x_ref[...], rest)
        e = jnp.exp(logits - jnp.max(logits, axis=-1, keepdims=True))
        probs = e / jnp.sum(e, axis=-1, keepdims=True)
        gate = jnp.sum(jnp.where(hot, probs, 0.0), axis=-1, keepdims=True)
        probs_ref[...] = probs
        gate_ref[...] = gate
        deo_ref[...] = (gate * c_ref[...].astype(f32)).astype(bf16)

    pre_ref[...] = dot(x_ref[...], w_in_ref[...])
    up_ref[...] = contract_last(deo_ref[...], w_out_ref[...])
    for r in range(0, rows, chunk):
        part = slice(r, r + chunk)
        u = pre_ref[part, :]
        up = up_ref[part, :]
        square = u * u
        t = jnp.tanh(gelu_scale * u * (1.0 + gelu_cubic * square))
        side = 0.5 * (1.0 + t)
        hid = u * side
        slope = side + (0.5 * gelu_scale) * u * (1.0 - t * t) * (1.0 + (3.0 * gelu_cubic) * square)
        hid_ref[part, :] = hid.astype(bf16)
        dpre_ref[part, :] = (up * slope).astype(bf16)
        inner = jnp.sum(hid * up, axis=-1, keepdims=True)
        before = jnp.where(step == 0, 0.0, inner_ref[part, :])
        inner_ref[part, :] = before + inner
    part = contract_last(dpre_ref[...], w_in_ref[...])

    @pl.when(step == 0)
    def _():
        total_ref[...] = part

    @pl.when(step > 0)
    def _():
        total_ref[...] += part

    @pl.when(step == pl.num_programs(0) - 1)
    def _():
        dlog = inner_ref[...] * (hot.astype(f32) - probs_ref[...])
        dlog_ref[...] = dlog
        dx_ref[...] = (
            total_ref[...] + dot(dlog.astype(bf16), router_ref[...].astype(bf16))
        ).astype(bf16)


def expert(x, c, w_in, w_out, router, mine):
    rows, width = x.shape
    hidden = w_in.shape[1]
    experts = router.shape[0]
    step = 512 if hidden % 512 == 0 else hidden
    return pl.pallas_call(
        expert_kernel,
        grid=(hidden // step,),
        in_specs=[
            whole((rows, width)), whole((rows, width)),
            pl.BlockSpec((width, step), lambda j: (0, j)),
            pl.BlockSpec((step, width), lambda j: (j, 0)),
            whole((experts, width)), scalars(),
        ],
        out_specs=[
            whole((rows, width)),
            pl.BlockSpec((rows, step), lambda j: (0, j)),
            pl.BlockSpec((rows, step), lambda j: (0, j)),
            whole((rows, width)), whole((rows, 1)), whole((rows, experts)),
        ],
        out_shape=[
            jax.ShapeDtypeStruct((rows, width), bf16),
            jax.ShapeDtypeStruct((rows, hidden), bf16),
            jax.ShapeDtypeStruct((rows, hidden), bf16),
            jax.ShapeDtypeStruct((rows, width), bf16),
            jax.ShapeDtypeStruct((rows, 1), f32),
            jax.ShapeDtypeStruct((rows, experts), f32),
        ],
        scratch_shapes=[
            pltpu.VMEM((rows, step), f32),
            pltpu.VMEM((rows, step), f32),
            pltpu.VMEM((rows, experts), f32),
            pltpu.VMEM((rows, 1), f32),
            pltpu.VMEM((rows, width), f32),
        ],
        compiler_params=params(58),
        cost_estimate=cost(4_500_000_000, 12_000_000),
        name="expert",
    )(x, c, w_in, w_out, router, mine)


def exchange(value, count, bit):
    return lax.ppermute(value, "dp", [(i, i ^ (1 << bit)) for i in range(count)])


def add(left, right):
    return (left.astype(f32) + right.astype(f32)).astype(left.dtype)


def shards(
    count,
    hidden_in,
    norm1_gain,
    w_query,
    w_key,
    w_value,
    w_output,
    bias_table,
    bucket_ids,
    norm2_gain,
    router,
    w_in,
    w_out,
    expert_ids,
    slot_ids,
    out_grad,
):
    tokens, width = hidden_in.shape
    buckets, heads = bias_table.shape
    experts = router.shape[1]
    capacity = max(2, 5 * tokens // (4 * experts))
    places = experts * capacity
    bits = (count - 1).bit_length()
    swap = [(0, 1), (1, 0)]
    mp = lax.axis_index("mp").astype(jnp.int32)
    dp = lax.axis_index("dp").astype(jnp.int32)
    side = (dp & 1)[None]
    where = jnp.stack([mp] + [(dp >> bit) & 1 for bit in range(bits)])

    def swapped(value):
        return lax.ppermute(value, "mp", swap)

    def to_experts(rows):
        block = rows.reshape(experts, capacity, -1)
        return lax.all_to_all(block, "dp", split_axis=0, concat_axis=0, tiled=True).reshape(
            places, -1
        )

    slot_row = (expert_ids[None, :], slot_ids[None, :])
    slot_column = (expert_ids * capacity + slot_ids)[:, None]

    w_near, _ = split(w_output, (dp & 1) == 0)
    w_near = swapped(w_near)
    c_here = to_experts(place(capacity, slot_row, out_grad, places))
    o, q, k, v, p, ids = attend(
        hidden_in, norm1_gain, w_query, w_key, w_value, bias_table.T, bucket_ids
    )
    o, w_near = lax.optimization_barrier((o, w_near))
    o_other = swapped(o)
    w_far = exchange(w_near, count, 0)
    hmid, x_send = middle(
        capacity, where, o, o_other, w_output, w_near, w_far, hidden_in, norm2_gain, slot_row, places
    )
    x_here = to_experts(x_send)

    dx, hid, dpre, deo, gate, dlog = expert(x_here, c_here, w_in[0], w_out[0], router.T, dp[None])
    dx_home = to_experts(dx)
    eo = (gate * dot(hid, w_out[0])).astype(bf16)
    eo_mine = jnp.where(mp == 0, eo[:, : width // 2], eo[:, width // 2 :])
    eo_other = swapped(jnp.where(mp == 0, eo[:, width // 2 :], eo[:, : width // 2]))
    grad_w_out = contract_rows(hid, deo)[None]
    grad_w_in = contract_rows(x_here, dpre)[None]
    grad_router = contract_rows(dlog, x_here.astype(f32), lax.Precision.HIGHEST)
    eo = add(eo_mine, eo_other)
    dx_home, grad_w_out, grad_w_in, grad_router = lax.optimization_barrier(
        (dx_home, grad_w_out, grad_w_in, grad_router)
    )

    low, high = pick(slot_column, dx_home, 2)
    low, high, eo = lax.optimization_barrier((low, high, eo))
    low_other = swapped(low)
    high_other = swapped(high)
    eo_home = to_experts(eo)
    before = middle_back(0, low, low_other, hmid, out_grad, norm2_gain, w_output)
    dh, da, do, grad_norm2 = middle_back(
        tokens // 2, high, high_other, hmid, out_grad, norm2_gain, w_output, before
    )
    dn1, keep, send = attend_back(
        side, do, q, k, v, p, w_query, w_key, w_value, o, da, hidden_in, norm1_gain, ids,
        grad_router, grad_norm2, buckets,
    )
    dn1, keep, send, eo_home = lax.optimization_barrier((dn1, keep, send, eo_home))
    dn1_other = swapped(dn1)

    local = q.shape[1]
    order_a = tuple(range(1, bits))
    order_b = (2, 1) + tuple(range(3, bits))
    got = exchange(send, count, 0)
    a, b = (keep[:local], got[:local]), (keep[local:], got[local:])
    for stage, (bit_a, bit_b) in enumerate(zip(order_a[:-1], order_b[:-1])):
        keep_a, send_a = split_sum(a, where[bit_a + 1] == 0)
        keep_b, send_b = split_sum(b, where[bit_b + 1] == 0)
        got_a = exchange(send_a, count, bit_a)
        got_b = exchange(send_b, count, bit_b)
        if stage == 0:
            (picked,) = pick(slot_column, eo_home, 1)
            got_a, got_b, picked = lax.optimization_barrier((got_a, got_b, picked))
        a, b = (keep_a, got_a), (keep_b, got_b)
    a, b = add(*a), add(*b)
    got_a = exchange(a, count, order_a[-1])
    got_b = exchange(b, count, order_b[-1])
    got_a, got_b, dn1_other = lax.optimization_barrier((got_a, got_b, dn1_other))
    picked_other = swapped(picked)
    a, b = add(a, got_a), add(b, got_b)
    for bit_a, bit_b in zip(order_a[-2::-1], order_b[-2::-1]):
        got_a = exchange(a, count, bit_a)
        got_b = exchange(b, count, bit_b)
        if bit_b == 1:
            grad_hidden, hidden_out = outputs(
                where, dn1, dn1_other, hidden_in, dh, norm1_gain, picked, picked_other, hmid
            )
            got_a, got_b, grad_hidden, hidden_out = lax.optimization_barrier(
                (got_a, got_b, grad_hidden, hidden_out)
            )
        a = pair_up(a, got_a, where[bit_a + 1] == 0)
        b = pair_up(b, got_b, where[bit_b + 1] == 0)
        if bit_b == 1:
            small = b[local // 2 :]
            b = b[: local // 2]
            small_other = swapped(small)
    a, b, small_other = lax.optimization_barrier((a, b, small_other))
    grad_q, grad_k, grad_v, grad_w_output, grad_router, grad_table, grad_norm1, grad_norm2 = unpack(
        where, a, exchange(a, count, 0), b, exchange(b, count, 0), small, small_other,
        experts, buckets, heads,
    )
    return (
        hidden_out,
        grad_hidden,
        grad_norm1,
        grad_q,
        grad_k,
        grad_v,
        grad_w_output,
        grad_table.T,
        grad_norm2,
        grad_router.T,
        grad_w_in,
        grad_w_out,
    )


def solution(mesh):
    return jax.shard_map(
        functools.partial(shards, mesh.shape["dp"]),
        mesh=mesh,
        in_specs=(
            P("dp", None),
            P(),
            P(None, "mp"),
            P(None, "mp"),
            P(None, "mp"),
            P("mp", None),
            P(None, "mp"),
            P(),
            P(),
            P(),
            P("dp", None, "mp"),
            P("dp", "mp", None),
            P("dp"),
            P("dp"),
            P("dp", None),
        ),
        out_specs=(
            P("dp", None),
            P("dp", None),
            P(),
            P(None, "mp"),
            P(None, "mp"),
            P(None, "mp"),
            P("mp", None),
            P(None, "mp"),
            P(),
            P(),
            P("dp", None, "mp"),
            P("dp", "mp", None),
        ),
        check_vma=False,
    )
```

```python
import functools

import jax
import jax.numpy as jnp
from jax import lax
from jax.experimental import pallas as pl
from jax.experimental.pallas import tpu as pltpu
from jax.sharding import PartitionSpec as P

epsilon = 1e-06
bf16 = jnp.bfloat16
f32 = jnp.float32
gelu_scale = 0.7978845608028654
gelu_cubic = 0.044715


def dot(left, right):
    return jnp.dot(left, right, preferred_element_type=f32)


def contract_last(left, right):
    return lax.dot_general(left, right, (((1,), (1,)), ((), ())), preferred_element_type=f32)


def contract_rows(left, right, precision=None):
    return lax.dot_general(
        left, right, (((0,), (0,)), ((), ())), preferred_element_type=f32, precision=precision
    )


def whole(shape):
    return pl.BlockSpec(shape, lambda *_: (0,) * len(shape))


def scalars():
    return pl.BlockSpec(memory_space=pltpu.SMEM)


def params(mib=62):
    return pltpu.CompilerParams(vmem_limit_bytes=mib * 1024 * 1024)


def cost(flops, moved):
    return pl.CostEstimate(flops=flops, bytes_accessed=moved, transcendentals=0)


def attend_kernel(
    x_ref, gain_ref, wq_ref, wk_ref, wv_ref, table_ref, first_ref, last_ref,
    o_ref, q_ref, k_ref, v_ref, p_ref, ids_ref, n_ref, bias_ref,
):
    pair = pl.program_id(0)
    length = x_ref.shape[0]
    buckets = table_ref.shape[1]
    half = o_ref.shape[1] // 2
    scale = half ** (-0.5)
    blocks = length // 128

    @pl.when(pair == 0)
    def _():
        x = x_ref[...].astype(f32)
        inverse = lax.rsqrt(jnp.mean(x * x, axis=-1, keepdims=True) + epsilon)
        n_ref[...] = (x * inverse * gain_ref[...][None, :]).astype(bf16)
        blank = jnp.zeros((8, length), jnp.int32)
        ahead = jnp.concatenate([jnp.broadcast_to(first_ref[0:1, :], (8, length)), blank], axis=1)
        behind = jnp.concatenate([jnp.broadcast_to(last_ref[7:8, :], (8, length)), blank], axis=1)
        place = lax.broadcasted_iota(jnp.int32, (8, 2 * length), 1)
        row = lax.broadcasted_iota(jnp.int32, (8, 2 * length), 0)
        line = jnp.where(place < length, behind, pltpu.roll(ahead, length - 1, 1))
        ids = line
        for r in range(1, 8):
            ids = jnp.where(row == r, pltpu.roll(line, r, 1), ids)
        ids_ref[...] = ids

    normed = n_ref[...]
    q = dot(normed, wq_ref[...]).astype(bf16)
    k = dot(normed, wk_ref[...]).astype(bf16)
    v = dot(normed, wv_ref[...]).astype(bf16)
    q_ref[...] = q
    k_ref[...] = k
    v_ref[...] = v
    ids = ids_ref[...]
    lane = lax.broadcasted_iota(jnp.int32, (length, 2 * half), 1)
    zero = jnp.zeros_like(q)
    out = None
    for h in range(2):
        head = 2 * pair + h
        mine = (lane < half) if h == 0 else (lane >= half)
        spread = jnp.zeros(ids.shape, f32)
        for b in range(buckets):
            spread = jnp.where(ids == b, table_ref[head, b], spread)
        for a in range(16):
            left = 127 - 8 * a
            bias_ref[8 * a : 8 * a + 8, :] = pltpu.roll(spread, 2 * length - left, 1)
        q_head = jnp.where(mine, q, zero)
        for i in range(blocks):
            rows = slice(128 * i, 128 * i + 128)
            start = 128 * (blocks - 1 - i)
            s = contract_last(q_head[rows], k) * scale + bias_ref[:, start : start + length]
            e = jnp.exp(s - jnp.max(s, axis=-1, keepdims=True))
            p = e * (1.0 / jnp.sum(e, axis=-1, keepdims=True))
            p_ref[h, rows, :] = p.astype(bf16)
        part = dot(p_ref[h], jnp.where(mine, v, zero))
        out = part if out is None else out + part
    o_ref[...] = out.astype(bf16)


def attend(x, gain, wq, wk, wv, table, bucket_ids):
    length, width = x.shape
    local = wq.shape[1]
    heads = table.shape[0]
    span = 2 * local // heads
    column = pl.BlockSpec((length, span), lambda j: (0, j))
    weight = pl.BlockSpec((width, span), lambda j: (0, j))
    thin = jax.ShapeDtypeStruct((length, local), bf16)
    return pl.pallas_call(
        attend_kernel,
        grid=(heads // 2,),
        in_specs=[
            whole((length, width)), whole((width,)), weight, weight, weight, scalars(),
            pl.BlockSpec((8, length), lambda j: (0, 0)),
            pl.BlockSpec((8, length), lambda j: (length // 8 - 1, 0)),
        ],
        out_specs=[
            column, column, column, column,
            pl.BlockSpec((2, length, length), lambda j: (j, 0, 0)),
            whole((8, 2 * length)),
        ],
        out_shape=[
            thin, thin, thin, thin,
            jax.ShapeDtypeStruct((heads, length, length), bf16),
            jax.ShapeDtypeStruct((8, 2 * length), jnp.int32),
        ],
        scratch_shapes=[pltpu.VMEM((length, width), bf16), pltpu.VMEM((128, 2 * length), f32)],
        compiler_params=params(),
        cost_estimate=cost(9_000_000_000, 9_000_000),
        name="attend",
    )(x, gain, wq, wk, wv, table, bucket_ids, bucket_ids)


def attend_back_kernel(
    buckets, side_ref, do_ref, q_ref, k_ref, v_ref, p_ref, wq_ref, wk_ref, wv_ref,
    o_ref, da_ref, x_ref, gain_ref, ids_ref, router_ref, norm2_ref,
    dn_ref, keep_ref, send_ref,
    ds_ref, acc_ref, total_ref, n_ref, small_ref,
):
    pair = pl.program_id(0)
    last = pl.num_programs(0) - 1
    length = do_ref.shape[0]
    span = do_ref.shape[1]
    half = span // 2
    scale = half ** (-0.5)
    blocks = length // 128
    experts = router_ref.shape[0]
    extra = small_ref.shape[0]
    local = keep_ref.shape[0] // 2 - extra
    quarter = local // 2
    even = side_ref[0] == 0

    @pl.when(pair == 0)
    def _():
        x = x_ref[...].astype(f32)
        inverse = lax.rsqrt(jnp.mean(x * x, axis=-1, keepdims=True) + epsilon)
        n_ref[...] = (x * inverse * gain_ref[...][None, :]).astype(bf16)
        small_ref[...] = jnp.zeros_like(small_ref)
        small_ref[0:experts, :] = router_ref[...]
        small_ref[experts + 1 : experts + 2, :] = norm2_ref[...]

    do = do_ref[...]
    q = q_ref[...]
    k = k_ref[...]
    v = v_ref[...]
    ids = ids_ref[...]
    q_turned = q.T
    do_turned = do.T
    lane = lax.broadcasted_iota(jnp.int32, (length, span), 1)
    zero = jnp.zeros_like(q)
    dq = None
    dk_parts = []
    dv_parts = []
    for h in range(2):
        mine = (lane < half) if h == 0 else (lane >= half)
        do_head = jnp.where(mine, do, zero)
        acc_ref[...] = jnp.zeros_like(acc_ref)
        for i in range(blocks):
            rows = slice(128 * i, 128 * i + 128)
            start = 128 * (blocks - 1 - i)
            p = p_ref[h, rows, :].astype(f32)
            dp = contract_last(do_head[rows], v)
            ds = p * (dp - jnp.sum(p * dp, axis=-1, keepdims=True))
            acc_ref[:, start : start + length] += ds
            ds_ref[rows, :] = ds.astype(bf16)
        ds_all = ds_ref[...]
        part = dot(ds_all, jnp.where(mine, k, zero))
        dq = part if dq is None else dq + part
        dk_parts.append(dot(q_turned[h * half : (h + 1) * half], ds_all))
        dv_parts.append(dot(do_turned[h * half : (h + 1) * half], p_ref[h]))
        diag = None
        for a in range(16):
            piece = pltpu.roll(acc_ref[8 * a : 8 * a + 8, :], 127 - 8 * a, 1)
            diag = piece if diag is None else diag + piece
        lines = []
        for b in range(buckets):
            hit = jnp.where(ids == b, diag, 0.0)
            fold = hit[:, 0:128]
            for y in range(1, 2 * length // 128):
                fold = fold + hit[:, 128 * y : 128 * y + 128]
            lines.append(jnp.sum(fold, axis=0, keepdims=True))
        lines.append(jnp.zeros((128 - buckets, 128), f32))
        sums = jnp.sum(jnp.concatenate(lines, axis=0).T, axis=0, keepdims=True)
        row = lax.broadcasted_iota(jnp.int32, (small_ref.shape[0], 128), 0)
        small_ref[:, 0:128] = jnp.where(
            row == experts + 2 + 2 * pair + h, sums, small_ref[:, 0:128]
        )
    dq_low = (dq * scale).astype(bf16)
    dk_turned = (jnp.concatenate(dk_parts, axis=0) * scale).astype(bf16)
    dv_turned = jnp.concatenate(dv_parts, axis=0).astype(bf16)
    part = (
        contract_last(dq_low, wq_ref[...])
        + contract_last(dk_turned.T, wk_ref[...])
        + contract_last(dv_turned.T, wv_ref[...])
    )
    normed = n_ref[...]
    here = pl.ds(pl.multiple_of(pair * span, span), span)
    grad_k = dot(dk_turned, normed).astype(bf16)
    grad_v = dot(dv_turned, normed).astype(bf16)
    keep_ref[here, :] = jnp.where(even, grad_k, grad_v)
    send_ref[here, :] = jnp.where(even, grad_v, grad_k)
    grad_q = dot(dq_low.T, normed).astype(bf16)
    grad_o = dot(o_ref[...].T, da_ref[...]).astype(bf16)
    keep = jnp.where(even, grad_q, grad_o)
    send = jnp.where(even, grad_o, grad_q)
    for i in range(0, span, 64):
        row = pair * span + i
        skip = jnp.where(row >= quarter, extra, 0)
        after = pl.ds(pl.multiple_of(local + row + skip, 32), 64)
        keep_ref[after, :] = keep[i : i + 64]
        send_ref[after, :] = send[i : i + 64]

    @pl.when(pair == 0)
    def _():
        total_ref[...] = part

    @pl.when(pair > 0)
    def _():
        total_ref[...] += part

    @pl.when(pair == last)
    def _():
        total = total_ref[...]
        dn_ref[...] = total.astype(bf16)
        x = x_ref[...].astype(f32)
        inverse = lax.rsqrt(jnp.mean(x * x, axis=-1, keepdims=True) + epsilon)
        small_ref[experts : experts + 1, :] = jnp.sum(
            total * x * inverse, axis=0, keepdims=True
        )
        small = small_ref[...].astype(bf16)
        for start in (local + quarter, 2 * local + extra):
            keep_ref[start : start + extra, :] = small
            send_ref[start : start + extra, :] = small


def small_rows(experts, heads):
    return -(-(experts + 2 + heads) // 32) * 32


def attend_back(side, do, q, k, v, p, wq, wk, wv, o, da, x, gain, ids, router, norm2, buckets):
    length, local = do.shape
    width = wq.shape[0]
    heads = p.shape[0]
    experts = router.shape[0]
    span = 2 * local // heads
    extra = small_rows(experts, heads)
    column = pl.BlockSpec((length, span), lambda j: (0, j))
    weight = pl.BlockSpec((width, span), lambda j: (0, j))
    part = jax.ShapeDtypeStruct((2 * (local + extra), width), bf16)
    return pl.pallas_call(
        functools.partial(attend_back_kernel, buckets),
        grid=(heads // 2,),
        in_specs=[
            scalars(), column, column, column, column,
            pl.BlockSpec((2, length, length), lambda j: (j, 0, 0)),
            weight, weight, weight, column,
            whole((length, width)), whole((length, width)), whole((width,)),
            whole(ids.shape), whole((experts, width)), whole((1, width)),
        ],
        out_specs=[
            whole((length, width)), whole(part.shape), whole(part.shape),
        ],
        out_shape=[
            jax.ShapeDtypeStruct((length, width), bf16), part, part,
        ],
        scratch_shapes=[
            pltpu.VMEM((length, length), bf16),
            pltpu.VMEM((128, 2 * length), f32),
            pltpu.VMEM((length, width), f32),
            pltpu.VMEM((length, width), bf16),
            pltpu.VMEM((extra, width), f32),
        ],
        compiler_params=params(),
        cost_estimate=cost(12_000_000_000, 9_000_000),
        name="attend_back",
    )(side, do, q, k, v, p, wq, wk, wv, o, da, x, gain, ids, router, norm2)


def hits(ids, count, axis):
    shape = (count, ids.shape[1]) if axis == 0 else (ids.shape[0], count)
    return jnp.where(lax.broadcasted_iota(jnp.int32, shape, axis) == ids, 1.0, 0.0).astype(bf16)


def row_block(block, width, first=0):
    return pl.BlockSpec((block, width), lambda i: (first + i, 0))


def row_block(block, width, first=0):
    return pl.BlockSpec((block, width), lambda i: (first + i, 0))


def place_kernel(capacity, expert_ref, slot_ref, rows_ref, out_ref):
    ids = expert_ref[...] * capacity + slot_ref[...]
    out_ref[...] = dot(hits(ids, out_ref.shape[0], 0), rows_ref[...]).astype(bf16)


def place(capacity, ids, rows, places):
    return pl.pallas_call(
        functools.partial(place_kernel, capacity),
        out_shape=jax.ShapeDtypeStruct((places, rows.shape[1]), bf16),
        compiler_params=params(),
        cost_estimate=cost(1_000_000_000, 3_000_000),
        name="place",
    )(*ids, rows)


def pick_kernel(ids_ref, slots_ref, *out_refs):
    first = 0
    for out_ref in out_refs:
        count = out_ref.shape[0]
        ids = ids_ref[first : first + count, :]
        out_ref[...] = dot(hits(ids, slots_ref.shape[0], 1), slots_ref[...]).astype(bf16)
        first += count


def pick(ids, slots, *counts):
    return pl.pallas_call(
        pick_kernel,
        out_shape=[jax.ShapeDtypeStruct((n, slots.shape[1]), bf16) for n in counts],
        compiler_params=params(16),
        cost_estimate=cost(1_000_000_000, 3_000_000),
        name="pick",
    )(ids, slots)


def middle_kernel(
    capacity, place_ref, o_ref, o_other_ref, w_ref, w_near_ref, w_far_ref, x_ref, gain_ref,
    expert_ref, slot_ref, hmid_ref, out_ref,
):
    low = place_ref[0] == 0
    even = place_ref[1] == 0
    o, o_other = o_ref[...], o_other_ref[...]
    w, near, far = w_ref[...], w_near_ref[...], w_far_ref[...]
    w_other = jnp.concatenate([jnp.where(even, near, far), jnp.where(even, far, near)], axis=0)
    heads = jnp.concatenate([jnp.where(low, o, o_other), jnp.where(low, o_other, o)], axis=1)
    weight = jnp.concatenate([jnp.where(low, w, w_other), jnp.where(low, w_other, w)], axis=0)
    hmid = x_ref[...].astype(f32) + dot(heads, weight)
    hmid_ref[...] = hmid
    inverse = lax.rsqrt(jnp.mean(hmid * hmid, axis=-1, keepdims=True) + epsilon)
    normed = (hmid * inverse * gain_ref[...][None, :]).astype(bf16)
    ids = expert_ref[...] * capacity + slot_ref[...]
    out_ref[...] = dot(hits(ids, out_ref.shape[0], 0), normed).astype(bf16)


def middle(capacity, where, o, o_other, w, w_near, w_far, x, gain, ids, places):
    return pl.pallas_call(
        functools.partial(middle_kernel, capacity),
        in_specs=[scalars()] + [pl.BlockSpec(memory_space=pltpu.VMEM)] * 9,
        out_shape=[
            jax.ShapeDtypeStruct(x.shape, f32),
            jax.ShapeDtypeStruct((places, x.shape[1]), bf16),
        ],
        compiler_params=params(58),
        cost_estimate=cost(2_000_000_000, 6_000_000),
        name="middle",
    )(where, o, o_other, w, w_near, w_far, x, gain, *ids)


def middle_back_kernel(
    own_ref, got_ref, hmid_ref, c_ref, gain_ref, w_ref, *refs
):
    dh_ref, da_ref, do_ref, norm_ref = refs[-4:]
    hmid = hmid_ref[...]
    dn = own_ref[...].astype(f32) + got_ref[...].astype(f32)
    inverse = lax.rsqrt(jnp.mean(hmid * hmid, axis=-1, keepdims=True) + epsilon)
    scaled = dn * gain_ref[...][None, :]
    inner = jnp.mean(scaled * hmid, axis=-1, keepdims=True)
    dh = c_ref[...].astype(f32) + inverse * scaled - hmid * (inverse * inverse * inverse * inner)
    dh_ref[...] = dh
    da = dh.astype(bf16)
    da_ref[...] = da
    do_ref[...] = contract_last(da, w_ref[...]).astype(bf16)
    norm = jnp.sum(dn * hmid * inverse, axis=0, keepdims=True)
    before = refs[3][...] if len(refs) > 4 else jnp.zeros_like(norm)

    @pl.when(pl.program_id(0) == 0)
    def _():
        norm_ref[...] = before + norm

    @pl.when(pl.program_id(0) > 0)
    def _():
        norm_ref[...] += norm


def middle_back(first, own, got, hmid, c, gain, w, before=()):
    count, width = own.shape
    tokens = hmid.shape[0]
    local = w.shape[0]
    block = count
    here = first // block
    anywhere = pl.BlockSpec(memory_space=pl.ANY)
    return pl.pallas_call(
        middle_back_kernel,
        grid=(count // block,),
        in_specs=[
            row_block(block, width), row_block(block, width),
            row_block(block, width, here), row_block(block, width, here),
            whole(gain.shape), whole(w.shape),
        ] + ([anywhere] * 3 + [whole((1, width))] if before else []),
        out_specs=[
            row_block(block, width, here), row_block(block, width, here),
            row_block(block, local, here), whole((1, width)),
        ],
        out_shape=[
            jax.ShapeDtypeStruct((tokens, width), f32),
            jax.ShapeDtypeStruct((tokens, width), bf16),
            jax.ShapeDtypeStruct((tokens, local), bf16),
            jax.ShapeDtypeStruct((1, width), f32),
        ],
        input_output_aliases={6: 0, 7: 1, 8: 2} if before else {},
        compiler_params=params(58),
        cost_estimate=cost(1_000_000_000, 6_000_000),
        name="middle_back",
    )(own, got, hmid, c, gain, w, *before)


def input_back_kernel(own_ref, got_ref, x_ref, dh_ref, gain_ref, grad_ref):
    x = x_ref[...].astype(f32)
    dn = own_ref[...].astype(f32) + got_ref[...].astype(f32)
    inverse = lax.rsqrt(jnp.mean(x * x, axis=-1, keepdims=True) + epsilon)
    scaled = dn * gain_ref[...][None, :]
    inner = jnp.mean(scaled * x, axis=-1, keepdims=True)
    grad_ref[...] = dh_ref[...] + inverse * scaled - x * (inverse * inverse * inverse * inner)


def input_back(own, got, x, dh, gain):
    return pl.pallas_call(
        input_back_kernel,
        out_shape=jax.ShapeDtypeStruct(dh.shape, f32),
        compiler_params=params(58),
        cost_estimate=cost(100_000_000, 6_000_000),
        name="input_back",
    )(own, got, x, dh, gain)


def finish_kernel(place_ref, y_ref, y_other_ref, hmid_ref, out_ref):
    low = place_ref[0] == 0
    y, y_other = y_ref[...], y_other_ref[...]
    moved = jnp.concatenate([jnp.where(low, y, y_other), jnp.where(low, y_other, y)], axis=1)
    out_ref[...] = (hmid_ref[...] + moved.astype(f32)).astype(bf16)


def finish(where, y, y_other, hmid):
    return pl.pallas_call(
        finish_kernel,
        in_specs=[scalars()] + [pl.BlockSpec(memory_space=pltpu.VMEM)] * 3,
        out_shape=jax.ShapeDtypeStruct(hmid.shape, bf16),
        compiler_params=params(58),
        cost_estimate=cost(1_000_000, 4_000_000),
        name="finish",
    )(where, y, y_other, hmid)


def split(value, low):
    n = value.shape[0] // 2
    first, second = value[:n], value[n:]
    return jnp.where(low, first, second), jnp.where(low, second, first)


def split_sum(pair, low):
    (keep, send), (got_keep, got_send) = split(pair[0], low), split(pair[1], low)
    return add(keep, got_keep), add(send, got_send)


def pair_up(value, got, low):
    return jnp.concatenate([jnp.where(low, value, got), jnp.where(low, got, value)], axis=0)


def unpack_kernel(
    experts, place_ref, a_ref, a_got_ref, b_ref, b_got_ref, small_ref, s_got_ref,
    q_ref, k_ref, v_ref, o_ref, router_ref, table_ref, norm1_ref, norm2_ref,
):
    even = place_ref[1] == 0
    heads, buckets = table_ref.shape
    a, a_got = a_ref[...], a_got_ref[...]
    b, b_got = b_ref[...], b_got_ref[...]
    k_ref[...] = jnp.where(even, a, a_got).T.astype(f32)
    v_ref[...] = jnp.where(even, a_got, a).T.astype(f32)
    q_ref[...] = jnp.where(even, b, b_got).T.astype(f32)
    o_ref[...] = jnp.where(even, b_got, b).astype(f32)
    small = small_ref[...].astype(f32)
    both = small + s_got_ref[...].astype(f32)
    router_ref[...] = both[:experts]
    norm1_ref[...] = both[experts]
    norm2_ref[...] = small[experts + 1]
    table_ref[...] = small[experts + 2 : experts + 2 + heads, :buckets]


def unpack(where, a, a_got, b, b_got, small, s_got, experts, buckets, heads):
    local, width = a.shape
    turned = jax.ShapeDtypeStruct((width, local), f32)
    flat = jax.ShapeDtypeStruct((width,), f32)
    return pl.pallas_call(
        functools.partial(unpack_kernel, experts),
        in_specs=[scalars()] + [pl.BlockSpec(memory_space=pltpu.VMEM)] * 6,
        out_shape=[
            turned, turned, turned,
            jax.ShapeDtypeStruct((local, width), f32),
            jax.ShapeDtypeStruct((experts, width), f32),
            jax.ShapeDtypeStruct((heads, buckets), f32),
            flat, flat,
        ],
        compiler_params=params(24),
        cost_estimate=cost(100_000_000, 8_000_000),
        name="unpack",
    )(where, a, a_got, b, b_got, small, s_got)


def expert_kernel(
    x_ref, c_ref, w_in_ref, w_out_ref, router_ref, mine_ref,
    dx_ref, hid_ref, dpre_ref, deo_ref, gate_ref, dlog_ref,
    pre_ref, up_ref, probs_ref, inner_ref, total_ref,
):
    step = pl.program_id(0)
    rows = x_ref.shape[0]
    chunk = 64
    hot = lax.broadcasted_iota(jnp.int32, probs_ref.shape, 1) == mine_ref[0]

    @pl.when(step == 0)
    def _():
        router = router_ref[...]
        high = router.astype(bf16)
        rest = (router - high.astype(f32)).astype(bf16)
        logits = contract_last(x_ref[...], high) + contract_last(x_ref[...], rest)
        e = jnp.exp(logits - jnp.max(logits, axis=-1, keepdims=True))
        probs = e / jnp.sum(e, axis=-1, keepdims=True)
        gate = jnp.sum(jnp.where(hot, probs, 0.0), axis=-1, keepdims=True)
        probs_ref[...] = probs
        gate_ref[...] = gate
        deo_ref[...] = (gate * c_ref[...].astype(f32)).astype(bf16)

    pre_ref[...] = dot(x_ref[...], w_in_ref[...])
    up_ref[...] = contract_last(deo_ref[...], w_out_ref[...])
    for r in range(0, rows, chunk):
        part = slice(r, r + chunk)
        u = pre_ref[part, :]
        up = up_ref[part, :]
        square = u * u
        t = jnp.tanh(gelu_scale * u * (1.0 + gelu_cubic * square))
        side = 0.5 * (1.0 + t)
        hid = u * side
        slope = side + (0.5 * gelu_scale) * u * (1.0 - t * t) * (1.0 + (3.0 * gelu_cubic) * square)
        hid_ref[part, :] = hid.astype(bf16)
        dpre_ref[part, :] = (up * slope).astype(bf16)
        inner = jnp.sum(hid * up, axis=-1, keepdims=True)
        before = jnp.where(step == 0, 0.0, inner_ref[part, :])
        inner_ref[part, :] = before + inner
    part = contract_last(dpre_ref[...], w_in_ref[...])

    @pl.when(step == 0)
    def _():
        total_ref[...] = part

    @pl.when(step > 0)
    def _():
        total_ref[...] += part

    @pl.when(step == pl.num_programs(0) - 1)
    def _():
        dlog = inner_ref[...] * (hot.astype(f32) - probs_ref[...])
        dlog_ref[...] = dlog
        dx_ref[...] = (
            total_ref[...] + dot(dlog.astype(bf16), router_ref[...].astype(bf16))
        ).astype(bf16)


def expert(x, c, w_in, w_out, router, mine):
    rows, width = x.shape
    hidden = w_in.shape[1]
    experts = router.shape[0]
    step = 512 if hidden % 512 == 0 else hidden
    return pl.pallas_call(
        expert_kernel,
        grid=(hidden // step,),
        in_specs=[
            whole((rows, width)), whole((rows, width)),
            pl.BlockSpec((width, step), lambda j: (0, j)),
            pl.BlockSpec((step, width), lambda j: (j, 0)),
            whole((experts, width)), scalars(),
        ],
        out_specs=[
            whole((rows, width)),
            pl.BlockSpec((rows, step), lambda j: (0, j)),
            pl.BlockSpec((rows, step), lambda j: (0, j)),
            whole((rows, width)), whole((rows, 1)), whole((rows, experts)),
        ],
        out_shape=[
            jax.ShapeDtypeStruct((rows, width), bf16),
            jax.ShapeDtypeStruct((rows, hidden), bf16),
            jax.ShapeDtypeStruct((rows, hidden), bf16),
            jax.ShapeDtypeStruct((rows, width), bf16),
            jax.ShapeDtypeStruct((rows, 1), f32),
            jax.ShapeDtypeStruct((rows, experts), f32),
        ],
        scratch_shapes=[
            pltpu.VMEM((rows, step), f32),
            pltpu.VMEM((rows, step), f32),
            pltpu.VMEM((rows, experts), f32),
            pltpu.VMEM((rows, 1), f32),
            pltpu.VMEM((rows, width), f32),
        ],
        compiler_params=params(58),
        cost_estimate=cost(4_500_000_000, 12_000_000),
        name="expert",
    )(x, c, w_in, w_out, router, mine)


def exchange(value, count, bit):
    return lax.ppermute(value, "dp", [(i, i ^ (1 << bit)) for i in range(count)])


def add(left, right):
    return (left.astype(f32) + right.astype(f32)).astype(left.dtype)


def shards(
    count,
    hidden_in,
    norm1_gain,
    w_query,
    w_key,
    w_value,
    w_output,
    bias_table,
    bucket_ids,
    norm2_gain,
    router,
    w_in,
    w_out,
    expert_ids,
    slot_ids,
    out_grad,
):
    tokens, width = hidden_in.shape
    buckets, heads = bias_table.shape
    experts = router.shape[1]
    capacity = max(2, 5 * tokens // (4 * experts))
    places = experts * capacity
    bits = (count - 1).bit_length()
    swap = [(0, 1), (1, 0)]
    mp = lax.axis_index("mp").astype(jnp.int32)
    dp = lax.axis_index("dp").astype(jnp.int32)
    side = (dp & 1)[None]
    where = jnp.stack([mp] + [(dp >> bit) & 1 for bit in range(bits)])

    def swapped(value):
        return lax.ppermute(value, "mp", swap)

    def to_experts(rows):
        block = rows.reshape(experts, capacity, -1)
        return lax.all_to_all(block, "dp", split_axis=0, concat_axis=0, tiled=True).reshape(
            places, -1
        )

    slot_row = (expert_ids[None, :], slot_ids[None, :])
    slot_column = (expert_ids * capacity + slot_ids)[:, None]

    w_near, _ = split(w_output, (dp & 1) == 0)
    w_near = swapped(w_near)
    c_here = to_experts(place(capacity, slot_row, out_grad, places))
    o, q, k, v, p, ids = attend(
        hidden_in, norm1_gain, w_query, w_key, w_value, bias_table.T, bucket_ids
    )
    o, w_near = lax.optimization_barrier((o, w_near))
    o_other = swapped(o)
    w_far = exchange(w_near, count, 0)
    hmid, x_send = middle(
        capacity, where, o, o_other, w_output, w_near, w_far, hidden_in, norm2_gain, slot_row, places
    )
    x_here = to_experts(x_send)

    dx, hid, dpre, deo, gate, dlog = expert(x_here, c_here, w_in[0], w_out[0], router.T, dp[None])
    dx_home = to_experts(dx)
    eo = (gate * dot(hid, w_out[0])).astype(bf16)
    eo_mine = jnp.where(mp == 0, eo[:, : width // 2], eo[:, width // 2 :])
    eo_other = swapped(jnp.where(mp == 0, eo[:, width // 2 :], eo[:, : width // 2]))
    grad_w_out = contract_rows(hid, deo)[None]
    grad_w_in = contract_rows(x_here, dpre)[None]
    grad_router = contract_rows(dlog, x_here.astype(f32), lax.Precision.HIGHEST)
    eo = add(eo_mine, eo_other)
    dx_home, grad_w_out, grad_w_in, grad_router = lax.optimization_barrier(
        (dx_home, grad_w_out, grad_w_in, grad_router)
    )

    first = 3 * tokens // 4
    low, high = pick(slot_column, dx_home, first, tokens - first)
    low, high, eo = lax.optimization_barrier((low, high, eo))
    low_other = swapped(low)
    high_other = swapped(high)
    eo_home = to_experts(eo)
    before = middle_back(0, low, low_other, hmid, out_grad, norm2_gain, w_output)
    dh, da, do, grad_norm2 = middle_back(
        first, high, high_other, hmid, out_grad, norm2_gain, w_output, before
    )
    dn1, keep, send = attend_back(
        side, do, q, k, v, p, w_query, w_key, w_value, o, da, hidden_in, norm1_gain, ids,
        grad_router, grad_norm2, buckets,
    )
    dn1, keep, send, eo_home = lax.optimization_barrier((dn1, keep, send, eo_home))
    dn1_other = swapped(dn1)

    local = q.shape[1]
    order_a = tuple(range(1, bits))
    order_b = (2, 1) + tuple(range(3, bits))
    got = exchange(send, count, 0)
    a, b = (keep[:local], got[:local]), (keep[local:], got[local:])
    for stage, (bit_a, bit_b) in enumerate(zip(order_a[:-1], order_b[:-1])):
        keep_a, send_a = split_sum(a, where[bit_a + 1] == 0)
        keep_b, send_b = split_sum(b, where[bit_b + 1] == 0)
        got_a = exchange(send_a, count, bit_a)
        got_b = exchange(send_b, count, bit_b)
        if stage == 0:
            (picked,) = pick(slot_column, eo_home, tokens)
            got_a, got_b, picked = lax.optimization_barrier((got_a, got_b, picked))
        a, b = (keep_a, got_a), (keep_b, got_b)
    a, b = add(*a), add(*b)
    got_a = exchange(a, count, order_a[-1])
    got_b = exchange(b, count, order_b[-1])
    grad_hidden = input_back(dn1, dn1_other, hidden_in, dh, norm1_gain)
    got_a, got_b, grad_hidden = lax.optimization_barrier((got_a, got_b, grad_hidden))
    picked_other = swapped(picked)
    a, b = add(a, got_a), add(b, got_b)
    for bit_a, bit_b in zip(order_a[-2::-1], order_b[-2::-1]):
        got_a = exchange(a, count, bit_a)
        got_b = exchange(b, count, bit_b)
        a = pair_up(a, got_a, where[bit_a + 1] == 0)
        b = pair_up(b, got_b, where[bit_b + 1] == 0)
        if bit_b == 1:
            small = b[local // 2 :]
            b = b[: local // 2]
            small_other = swapped(small)
    hidden_out = finish(where, picked, picked_other, hmid)
    a, b, small_other, hidden_out = lax.optimization_barrier((a, b, small_other, hidden_out))
    grad_q, grad_k, grad_v, grad_w_output, grad_router, grad_table, grad_norm1, grad_norm2 = unpack(
        where, a, exchange(a, count, 0), b, exchange(b, count, 0), small, small_other,
        experts, buckets, heads,
    )
    return (
        hidden_out,
        grad_hidden,
        grad_norm1,
        grad_q,
        grad_k,
        grad_v,
        grad_w_output,
        grad_table.T,
        grad_norm2,
        grad_router.T,
        grad_w_in,
        grad_w_out,
    )


def solution(mesh):
    return jax.shard_map(
        functools.partial(shards, mesh.shape["dp"]),
        mesh=mesh,
        in_specs=(
            P("dp", None),
            P(),
            P(None, "mp"),
            P(None, "mp"),
            P(None, "mp"),
            P("mp", None),
            P(None, "mp"),
            P(),
            P(),
            P(),
            P("dp", None, "mp"),
            P("dp", "mp", None),
            P("dp"),
            P("dp"),
            P("dp", None),
        ),
        out_specs=(
            P("dp", None),
            P("dp", None),
            P(),
            P(None, "mp"),
            P(None, "mp"),
            P(None, "mp"),
            P("mp", None),
            P(None, "mp"),
            P(),
            P(),
            P("dp", None, "mp"),
            P("dp", "mp", None),
        ),
        check_vma=False,
    )
```

```python
import functools

import jax
import jax.numpy as jnp
from jax import lax
from jax.experimental import pallas as pl
from jax.experimental.pallas import tpu as pltpu
from jax.sharding import PartitionSpec as P

epsilon = 1e-06
bf16 = jnp.bfloat16
f32 = jnp.float32
gelu_scale = 0.7978845608028654
gelu_cubic = 0.044715


def dot(left, right):
    return jnp.dot(left, right, preferred_element_type=f32)


def contract_last(left, right):
    return lax.dot_general(left, right, (((1,), (1,)), ((), ())), preferred_element_type=f32)


def contract_rows(left, right, precision=None):
    return lax.dot_general(
        left, right, (((0,), (0,)), ((), ())), preferred_element_type=f32, precision=precision
    )


def whole(shape):
    return pl.BlockSpec(shape, lambda *_: (0,) * len(shape))


def scalars():
    return pl.BlockSpec(memory_space=pltpu.SMEM)


def params(mib=62):
    return pltpu.CompilerParams(vmem_limit_bytes=mib * 1024 * 1024)


def cost(flops, moved):
    return pl.CostEstimate(flops=flops, bytes_accessed=moved, transcendentals=0)


def attend_kernel(
    x_ref, gain_ref, wq_ref, wk_ref, wv_ref, table_ref, first_ref, last_ref,
    o_ref, q_ref, k_ref, v_ref, p_ref, ids_ref, n_ref, bias_ref,
):
    pair = pl.program_id(0)
    length = x_ref.shape[0]
    buckets = table_ref.shape[1]
    half = o_ref.shape[1] // 2
    scale = half ** (-0.5)
    blocks = length // 128

    @pl.when(pair == 0)
    def _():
        x = x_ref[...].astype(f32)
        inverse = lax.rsqrt(jnp.mean(x * x, axis=-1, keepdims=True) + epsilon)
        n_ref[...] = (x * inverse * gain_ref[...][None, :]).astype(bf16)
        blank = jnp.zeros((8, length), jnp.int32)
        ahead = jnp.concatenate([jnp.broadcast_to(first_ref[0:1, :], (8, length)), blank], axis=1)
        behind = jnp.concatenate([jnp.broadcast_to(last_ref[7:8, :], (8, length)), blank], axis=1)
        place = lax.broadcasted_iota(jnp.int32, (8, 2 * length), 1)
        row = lax.broadcasted_iota(jnp.int32, (8, 2 * length), 0)
        line = jnp.where(place < length, behind, pltpu.roll(ahead, length - 1, 1))
        ids = line
        for r in range(1, 8):
            ids = jnp.where(row == r, pltpu.roll(line, r, 1), ids)
        ids_ref[...] = ids

    normed = n_ref[...]
    span = 2 * half
    weight = jnp.concatenate([wq_ref[...], wk_ref[...], wv_ref[...]], axis=1)
    qkv = dot(normed, weight).astype(bf16)
    q, k, v = qkv[:, :span], qkv[:, span : 2 * span], qkv[:, 2 * span :]
    q_ref[...] = q
    k_ref[...] = k
    v_ref[...] = v
    ids = ids_ref[...]
    lane = lax.broadcasted_iota(jnp.int32, (length, 2 * half), 1)
    zero = jnp.zeros_like(q)
    out = None
    for h in range(2):
        head = 2 * pair + h
        mine = (lane < half) if h == 0 else (lane >= half)
        spread = jnp.zeros(ids.shape, f32)
        for b in range(buckets):
            spread = jnp.where(ids == b, table_ref[head, b], spread)
        for a in range(16):
            left = 127 - 8 * a
            bias_ref[8 * a : 8 * a + 8, :] = pltpu.roll(spread, 2 * length - left, 1)
        q_head = jnp.where(mine, q, zero)
        for i in range(blocks):
            rows = slice(128 * i, 128 * i + 128)
            start = 128 * (blocks - 1 - i)
            s = contract_last(q_head[rows], k) * scale + bias_ref[:, start : start + length]
            e = jnp.exp(s - jnp.max(s, axis=-1, keepdims=True))
            p = e * (1.0 / jnp.sum(e, axis=-1, keepdims=True))
            p_ref[h, rows, :] = p.astype(bf16)
        part = dot(p_ref[h], jnp.where(mine, v, zero))
        out = part if out is None else out + part
    o_ref[...] = out.astype(bf16)


def attend(x, gain, wq, wk, wv, table, bucket_ids):
    length, width = x.shape
    local = wq.shape[1]
    heads = table.shape[0]
    span = 2 * local // heads
    column = pl.BlockSpec((length, span), lambda j: (0, j))
    weight = pl.BlockSpec((width, span), lambda j: (0, j))
    thin = jax.ShapeDtypeStruct((length, local), bf16)
    return pl.pallas_call(
        attend_kernel,
        grid=(heads // 2,),
        in_specs=[
            whole((length, width)), whole((width,)), weight, weight, weight, scalars(),
            pl.BlockSpec((8, length), lambda j: (0, 0)),
            pl.BlockSpec((8, length), lambda j: (length // 8 - 1, 0)),
        ],
        out_specs=[
            column, column, column, column,
            pl.BlockSpec((2, length, length), lambda j: (j, 0, 0)),
            whole((8, 2 * length)),
        ],
        out_shape=[
            thin, thin, thin, thin,
            jax.ShapeDtypeStruct((heads, length, length), bf16),
            jax.ShapeDtypeStruct((8, 2 * length), jnp.int32),
        ],
        scratch_shapes=[pltpu.VMEM((length, width), bf16), pltpu.VMEM((128, 2 * length), f32)],
        compiler_params=params(),
        cost_estimate=cost(9_000_000_000, 9_000_000),
        name="attend",
    )(x, gain, wq, wk, wv, table, bucket_ids, bucket_ids)


def attend_back_kernel(
    buckets, side_ref, do_ref, q_ref, k_ref, v_ref, p_ref, wq_ref, wk_ref, wv_ref,
    o_ref, da_ref, x_ref, gain_ref, ids_ref, router_ref, norm2_ref,
    dn_ref, keep_ref, send_ref,
    ds_ref, acc_ref, total_ref, n_ref, small_ref,
):
    pair = pl.program_id(0)
    last = pl.num_programs(0) - 1
    length = do_ref.shape[0]
    span = do_ref.shape[1]
    half = span // 2
    scale = half ** (-0.5)
    blocks = length // 128
    experts = router_ref.shape[0]
    extra = small_ref.shape[0]
    local = keep_ref.shape[0] // 2 - extra
    quarter = local // 2
    even = side_ref[0] == 0

    @pl.when(pair == 0)
    def _():
        x = x_ref[...].astype(f32)
        inverse = lax.rsqrt(jnp.mean(x * x, axis=-1, keepdims=True) + epsilon)
        n_ref[...] = (x * inverse * gain_ref[...][None, :]).astype(bf16)
        small_ref[...] = jnp.zeros_like(small_ref)
        small_ref[0:experts, :] = router_ref[...]
        small_ref[experts + 1 : experts + 2, :] = norm2_ref[...]

    do = do_ref[...]
    q = q_ref[...]
    k = k_ref[...]
    v = v_ref[...]
    ids = ids_ref[...]
    q_turned = q.T
    do_turned = do.T
    lane = lax.broadcasted_iota(jnp.int32, (length, span), 1)
    zero = jnp.zeros_like(q)
    dq = None
    dk_parts = []
    dv_parts = []
    for h in range(2):
        mine = (lane < half) if h == 0 else (lane >= half)
        do_head = jnp.where(mine, do, zero)
        acc_ref[...] = jnp.zeros_like(acc_ref)
        for i in range(blocks):
            rows = slice(128 * i, 128 * i + 128)
            start = 128 * (blocks - 1 - i)
            p = p_ref[h, rows, :].astype(f32)
            dp = contract_last(do_head[rows], v)
            ds = p * (dp - jnp.sum(p * dp, axis=-1, keepdims=True))
            acc_ref[:, start : start + length] += ds
            ds_ref[rows, :] = ds.astype(bf16)
        ds_all = ds_ref[...]
        part = dot(ds_all, jnp.where(mine, k, zero))
        dq = part if dq is None else dq + part
        dk_parts.append(dot(q_turned[h * half : (h + 1) * half], ds_all))
        dv_parts.append(dot(do_turned[h * half : (h + 1) * half], p_ref[h]))
        diag = None
        for a in range(16):
            piece = pltpu.roll(acc_ref[8 * a : 8 * a + 8, :], 127 - 8 * a, 1)
            diag = piece if diag is None else diag + piece
        lines = []
        for b in range(buckets):
            hit = jnp.where(ids == b, diag, 0.0)
            fold = hit[:, 0:128]
            for y in range(1, 2 * length // 128):
                fold = fold + hit[:, 128 * y : 128 * y + 128]
            lines.append(jnp.sum(fold, axis=0, keepdims=True))
        lines.append(jnp.zeros((128 - buckets, 128), f32))
        sums = jnp.sum(jnp.concatenate(lines, axis=0).T, axis=0, keepdims=True)
        row = lax.broadcasted_iota(jnp.int32, (small_ref.shape[0], 128), 0)
        small_ref[:, 0:128] = jnp.where(
            row == experts + 2 + 2 * pair + h, sums, small_ref[:, 0:128]
        )
    dq_low = (dq * scale).astype(bf16)
    dk_turned = (jnp.concatenate(dk_parts, axis=0) * scale).astype(bf16)
    dv_turned = jnp.concatenate(dv_parts, axis=0).astype(bf16)
    part = contract_last(
        jnp.concatenate([dq_low, dk_turned.T, dv_turned.T], axis=1),
        jnp.concatenate([wq_ref[...], wk_ref[...], wv_ref[...]], axis=1),
    )
    normed = n_ref[...]
    here = pl.ds(pl.multiple_of(pair * span, span), span)
    turned = jnp.concatenate([dk_turned, dv_turned, dq_low.T], axis=0)
    grads = dot(turned, normed).astype(bf16)
    grad_k, grad_v, grad_q = grads[:span], grads[span : 2 * span], grads[2 * span :]
    keep_ref[here, :] = jnp.where(even, grad_k, grad_v)
    send_ref[here, :] = jnp.where(even, grad_v, grad_k)
    grad_o = dot(o_ref[...].T, da_ref[...]).astype(bf16)
    keep = jnp.where(even, grad_q, grad_o)
    send = jnp.where(even, grad_o, grad_q)
    for i in range(0, span, 64):
        row = pair * span + i
        skip = jnp.where(row >= quarter, extra, 0)
        after = pl.ds(pl.multiple_of(local + row + skip, 32), 64)
        keep_ref[after, :] = keep[i : i + 64]
        send_ref[after, :] = send[i : i + 64]

    @pl.when(pair == 0)
    def _():
        total_ref[...] = part

    @pl.when(pair > 0)
    def _():
        total_ref[...] += part

    @pl.when(pair == last)
    def _():
        total = total_ref[...]
        dn_ref[...] = total.astype(bf16)
        x = x_ref[...].astype(f32)
        inverse = lax.rsqrt(jnp.mean(x * x, axis=-1, keepdims=True) + epsilon)
        small_ref[experts : experts + 1, :] = jnp.sum(
            total * x * inverse, axis=0, keepdims=True
        )
        small = small_ref[...].astype(bf16)
        for start in (local + quarter, 2 * local + extra):
            keep_ref[start : start + extra, :] = small
            send_ref[start : start + extra, :] = small


def small_rows(experts, heads):
    return -(-(experts + 2 + heads) // 32) * 32


def attend_back(side, do, q, k, v, p, wq, wk, wv, o, da, x, gain, ids, router, norm2, buckets):
    length, local = do.shape
    width = wq.shape[0]
    heads = p.shape[0]
    experts = router.shape[0]
    span = 2 * local // heads
    extra = small_rows(experts, heads)
    column = pl.BlockSpec((length, span), lambda j: (0, j))
    weight = pl.BlockSpec((width, span), lambda j: (0, j))
    part = jax.ShapeDtypeStruct((2 * (local + extra), width), bf16)
    return pl.pallas_call(
        functools.partial(attend_back_kernel, buckets),
        grid=(heads // 2,),
        in_specs=[
            scalars(), column, column, column, column,
            pl.BlockSpec((2, length, length), lambda j: (j, 0, 0)),
            weight, weight, weight, column,
            whole((length, width)), whole((length, width)), whole((width,)),
            whole(ids.shape), whole((experts, width)), whole((1, width)),
        ],
        out_specs=[
            whole((length, width)), whole(part.shape), whole(part.shape),
        ],
        out_shape=[
            jax.ShapeDtypeStruct((length, width), bf16), part, part,
        ],
        scratch_shapes=[
            pltpu.VMEM((length, length), bf16),
            pltpu.VMEM((128, 2 * length), f32),
            pltpu.VMEM((length, width), f32),
            pltpu.VMEM((length, width), bf16),
            pltpu.VMEM((extra, width), f32),
        ],
        compiler_params=params(),
        cost_estimate=cost(12_000_000_000, 9_000_000),
        name="attend_back",
    )(side, do, q, k, v, p, wq, wk, wv, o, da, x, gain, ids, router, norm2)


def hits(ids, count, axis):
    shape = (count, ids.shape[1]) if axis == 0 else (ids.shape[0], count)
    return jnp.where(lax.broadcasted_iota(jnp.int32, shape, axis) == ids, 1.0, 0.0).astype(bf16)


def row_block(block, width, first=0):
    return pl.BlockSpec((block, width), lambda i: (first + i, 0))


def row_block(block, width, first=0):
    return pl.BlockSpec((block, width), lambda i: (first + i, 0))


def place_kernel(capacity, expert_ref, slot_ref, rows_ref, out_ref):
    ids = expert_ref[...] * capacity + slot_ref[...]
    out_ref[...] = dot(hits(ids, out_ref.shape[0], 0), rows_ref[...]).astype(bf16)


def place(capacity, ids, rows, places):
    return pl.pallas_call(
        functools.partial(place_kernel, capacity),
        out_shape=jax.ShapeDtypeStruct((places, rows.shape[1]), bf16),
        compiler_params=params(),
        cost_estimate=cost(1_000_000_000, 3_000_000),
        name="place",
    )(*ids, rows)


def pick_kernel(ids_ref, slots_ref, *out_refs):
    first = 0
    for out_ref in out_refs:
        count = out_ref.shape[0]
        ids = ids_ref[first : first + count, :]
        out_ref[...] = dot(hits(ids, slots_ref.shape[0], 1), slots_ref[...]).astype(bf16)
        first += count


def pick(ids, slots, *counts):
    return pl.pallas_call(
        pick_kernel,
        out_shape=[jax.ShapeDtypeStruct((n, slots.shape[1]), bf16) for n in counts],
        compiler_params=params(16),
        cost_estimate=cost(1_000_000_000, 3_000_000),
        name="pick",
    )(ids, slots)


def middle_kernel(
    capacity, place_ref, o_ref, o_other_ref, w_ref, w_near_ref, w_far_ref, x_ref, gain_ref,
    expert_ref, slot_ref, hmid_ref, out_ref,
):
    low = place_ref[0] == 0
    even = place_ref[1] == 0
    o, o_other = o_ref[...], o_other_ref[...]
    w, near, far = w_ref[...], w_near_ref[...], w_far_ref[...]
    w_other = jnp.concatenate([jnp.where(even, near, far), jnp.where(even, far, near)], axis=0)
    heads = jnp.concatenate([jnp.where(low, o, o_other), jnp.where(low, o_other, o)], axis=1)
    weight = jnp.concatenate([jnp.where(low, w, w_other), jnp.where(low, w_other, w)], axis=0)
    hmid = x_ref[...].astype(f32) + dot(heads, weight)
    hmid_ref[...] = hmid
    inverse = lax.rsqrt(jnp.mean(hmid * hmid, axis=-1, keepdims=True) + epsilon)
    normed = (hmid * inverse * gain_ref[...][None, :]).astype(bf16)
    ids = expert_ref[...] * capacity + slot_ref[...]
    out_ref[...] = dot(hits(ids, out_ref.shape[0], 0), normed).astype(bf16)


def middle(capacity, where, o, o_other, w, w_near, w_far, x, gain, ids, places):
    return pl.pallas_call(
        functools.partial(middle_kernel, capacity),
        in_specs=[scalars()] + [pl.BlockSpec(memory_space=pltpu.VMEM)] * 9,
        out_shape=[
            jax.ShapeDtypeStruct(x.shape, f32),
            jax.ShapeDtypeStruct((places, x.shape[1]), bf16),
        ],
        compiler_params=params(58),
        cost_estimate=cost(2_000_000_000, 6_000_000),
        name="middle",
    )(where, o, o_other, w, w_near, w_far, x, gain, *ids)


def middle_back_kernel(
    own_ref, got_ref, hmid_ref, c_ref, gain_ref, w_ref, *refs
):
    dh_ref, da_ref, do_ref, norm_ref = refs[-4:]
    hmid = hmid_ref[...]
    dn = own_ref[...].astype(f32) + got_ref[...].astype(f32)
    inverse = lax.rsqrt(jnp.mean(hmid * hmid, axis=-1, keepdims=True) + epsilon)
    scaled = dn * gain_ref[...][None, :]
    inner = jnp.mean(scaled * hmid, axis=-1, keepdims=True)
    dh = c_ref[...].astype(f32) + inverse * scaled - hmid * (inverse * inverse * inverse * inner)
    dh_ref[...] = dh
    da = dh.astype(bf16)
    da_ref[...] = da
    do_ref[...] = contract_last(da, w_ref[...]).astype(bf16)
    norm = jnp.sum(dn * hmid * inverse, axis=0, keepdims=True)
    before = refs[3][...] if len(refs) > 4 else jnp.zeros_like(norm)

    @pl.when(pl.program_id(0) == 0)
    def _():
        norm_ref[...] = before + norm

    @pl.when(pl.program_id(0) > 0)
    def _():
        norm_ref[...] += norm


def middle_back(first, own, got, hmid, c, gain, w, before=()):
    count, width = own.shape
    tokens = hmid.shape[0]
    local = w.shape[0]
    block = count
    here = first // block
    anywhere = pl.BlockSpec(memory_space=pl.ANY)
    return pl.pallas_call(
        middle_back_kernel,
        grid=(count // block,),
        in_specs=[
            row_block(block, width), row_block(block, width),
            row_block(block, width, here), row_block(block, width, here),
            whole(gain.shape), whole(w.shape),
        ] + ([anywhere] * 3 + [whole((1, width))] if before else []),
        out_specs=[
            row_block(block, width, here), row_block(block, width, here),
            row_block(block, local, here), whole((1, width)),
        ],
        out_shape=[
            jax.ShapeDtypeStruct((tokens, width), f32),
            jax.ShapeDtypeStruct((tokens, width), bf16),
            jax.ShapeDtypeStruct((tokens, local), bf16),
            jax.ShapeDtypeStruct((1, width), f32),
        ],
        input_output_aliases={6: 0, 7: 1, 8: 2} if before else {},
        compiler_params=params(58),
        cost_estimate=cost(1_000_000_000, 6_000_000),
        name="middle_back",
    )(own, got, hmid, c, gain, w, *before)


def input_back_kernel(own_ref, got_ref, x_ref, dh_ref, gain_ref, grad_ref):
    x = x_ref[...].astype(f32)
    dn = own_ref[...].astype(f32) + got_ref[...].astype(f32)
    inverse = lax.rsqrt(jnp.mean(x * x, axis=-1, keepdims=True) + epsilon)
    scaled = dn * gain_ref[...][None, :]
    inner = jnp.mean(scaled * x, axis=-1, keepdims=True)
    grad_ref[...] = dh_ref[...] + inverse * scaled - x * (inverse * inverse * inverse * inner)


def input_back(own, got, x, dh, gain):
    return pl.pallas_call(
        input_back_kernel,
        out_shape=jax.ShapeDtypeStruct(dh.shape, f32),
        compiler_params=params(58),
        cost_estimate=cost(100_000_000, 6_000_000),
        name="input_back",
    )(own, got, x, dh, gain)


def finish_kernel(place_ref, y_ref, y_other_ref, hmid_ref, out_ref):
    low = place_ref[0] == 0
    y, y_other = y_ref[...], y_other_ref[...]
    moved = jnp.concatenate([jnp.where(low, y, y_other), jnp.where(low, y_other, y)], axis=1)
    out_ref[...] = (hmid_ref[...] + moved.astype(f32)).astype(bf16)


def finish(where, y, y_other, hmid):
    return pl.pallas_call(
        finish_kernel,
        in_specs=[scalars()] + [pl.BlockSpec(memory_space=pltpu.VMEM)] * 3,
        out_shape=jax.ShapeDtypeStruct(hmid.shape, bf16),
        compiler_params=params(58),
        cost_estimate=cost(1_000_000, 4_000_000),
        name="finish",
    )(where, y, y_other, hmid)


def split(value, low):
    n = value.shape[0] // 2
    first, second = value[:n], value[n:]
    return jnp.where(low, first, second), jnp.where(low, second, first)


def split_sum(pair, low):
    (keep, send), (got_keep, got_send) = split(pair[0], low), split(pair[1], low)
    return add(keep, got_keep), add(send, got_send)


def pair_up(value, got, low):
    return jnp.concatenate([jnp.where(low, value, got), jnp.where(low, got, value)], axis=0)


def unpack_kernel(
    experts, place_ref, a_ref, a_got_ref, b_ref, b_got_ref, small_ref, s_got_ref,
    q_ref, k_ref, v_ref, o_ref, router_ref, table_ref, norm1_ref, norm2_ref,
):
    even = place_ref[1] == 0
    heads, buckets = table_ref.shape
    a, a_got = a_ref[...], a_got_ref[...]
    b, b_got = b_ref[...], b_got_ref[...]
    k_ref[...] = jnp.where(even, a, a_got).T.astype(f32)
    v_ref[...] = jnp.where(even, a_got, a).T.astype(f32)
    q_ref[...] = jnp.where(even, b, b_got).T.astype(f32)
    o_ref[...] = jnp.where(even, b_got, b).astype(f32)
    small = small_ref[...].astype(f32)
    both = small + s_got_ref[...].astype(f32)
    router_ref[...] = both[:experts]
    norm1_ref[...] = both[experts]
    norm2_ref[...] = small[experts + 1]
    table_ref[...] = small[experts + 2 : experts + 2 + heads, :buckets]


def unpack(where, a, a_got, b, b_got, small, s_got, experts, buckets, heads):
    local, width = a.shape
    turned = jax.ShapeDtypeStruct((width, local), f32)
    flat = jax.ShapeDtypeStruct((width,), f32)
    return pl.pallas_call(
        functools.partial(unpack_kernel, experts),
        in_specs=[scalars()] + [pl.BlockSpec(memory_space=pltpu.VMEM)] * 6,
        out_shape=[
            turned, turned, turned,
            jax.ShapeDtypeStruct((local, width), f32),
            jax.ShapeDtypeStruct((experts, width), f32),
            jax.ShapeDtypeStruct((heads, buckets), f32),
            flat, flat,
        ],
        compiler_params=params(24),
        cost_estimate=cost(100_000_000, 8_000_000),
        name="unpack",
    )(where, a, a_got, b, b_got, small, s_got)


def expert_kernel(
    x_ref, c_ref, w_in_ref, w_out_ref, router_ref, mine_ref,
    dx_ref, hid_ref, dpre_ref, deo_ref, gate_ref, dlog_ref,
    pre_ref, up_ref, probs_ref, inner_ref, total_ref,
):
    step = pl.program_id(0)
    rows = x_ref.shape[0]
    chunk = 64
    hot = lax.broadcasted_iota(jnp.int32, probs_ref.shape, 1) == mine_ref[0]

    @pl.when(step == 0)
    def _():
        router = router_ref[...]
        high = router.astype(bf16)
        rest = (router - high.astype(f32)).astype(bf16)
        logits = contract_last(x_ref[...], high) + contract_last(x_ref[...], rest)
        e = jnp.exp(logits - jnp.max(logits, axis=-1, keepdims=True))
        probs = e / jnp.sum(e, axis=-1, keepdims=True)
        gate = jnp.sum(jnp.where(hot, probs, 0.0), axis=-1, keepdims=True)
        probs_ref[...] = probs
        gate_ref[...] = gate
        deo_ref[...] = (gate * c_ref[...].astype(f32)).astype(bf16)

    pre_ref[...] = dot(x_ref[...], w_in_ref[...])
    up_ref[...] = contract_last(deo_ref[...], w_out_ref[...])
    for r in range(0, rows, chunk):
        part = slice(r, r + chunk)
        u = pre_ref[part, :]
        up = up_ref[part, :]
        square = u * u
        t = jnp.tanh(gelu_scale * u * (1.0 + gelu_cubic * square))
        side = 0.5 * (1.0 + t)
        hid = u * side
        slope = side + (0.5 * gelu_scale) * u * (1.0 - t * t) * (1.0 + (3.0 * gelu_cubic) * square)
        hid_ref[part, :] = hid.astype(bf16)
        dpre_ref[part, :] = (up * slope).astype(bf16)
        inner = jnp.sum(hid * up, axis=-1, keepdims=True)
        before = jnp.where(step == 0, 0.0, inner_ref[part, :])
        inner_ref[part, :] = before + inner
    part = contract_last(dpre_ref[...], w_in_ref[...])

    @pl.when(step == 0)
    def _():
        total_ref[...] = part

    @pl.when(step > 0)
    def _():
        total_ref[...] += part

    @pl.when(step == pl.num_programs(0) - 1)
    def _():
        dlog = inner_ref[...] * (hot.astype(f32) - probs_ref[...])
        dlog_ref[...] = dlog
        dx_ref[...] = (
            total_ref[...] + dot(dlog.astype(bf16), router_ref[...].astype(bf16))
        ).astype(bf16)


def expert(x, c, w_in, w_out, router, mine):
    rows, width = x.shape
    hidden = w_in.shape[1]
    experts = router.shape[0]
    step = 512 if hidden % 512 == 0 else hidden
    return pl.pallas_call(
        expert_kernel,
        grid=(hidden // step,),
        in_specs=[
            whole((rows, width)), whole((rows, width)),
            pl.BlockSpec((width, step), lambda j: (0, j)),
            pl.BlockSpec((step, width), lambda j: (j, 0)),
            whole((experts, width)), scalars(),
        ],
        out_specs=[
            whole((rows, width)),
            pl.BlockSpec((rows, step), lambda j: (0, j)),
            pl.BlockSpec((rows, step), lambda j: (0, j)),
            whole((rows, width)), whole((rows, 1)), whole((rows, experts)),
        ],
        out_shape=[
            jax.ShapeDtypeStruct((rows, width), bf16),
            jax.ShapeDtypeStruct((rows, hidden), bf16),
            jax.ShapeDtypeStruct((rows, hidden), bf16),
            jax.ShapeDtypeStruct((rows, width), bf16),
            jax.ShapeDtypeStruct((rows, 1), f32),
            jax.ShapeDtypeStruct((rows, experts), f32),
        ],
        scratch_shapes=[
            pltpu.VMEM((rows, step), f32),
            pltpu.VMEM((rows, step), f32),
            pltpu.VMEM((rows, experts), f32),
            pltpu.VMEM((rows, 1), f32),
            pltpu.VMEM((rows, width), f32),
        ],
        compiler_params=params(58),
        cost_estimate=cost(4_500_000_000, 12_000_000),
        name="expert",
    )(x, c, w_in, w_out, router, mine)


def exchange(value, count, bit):
    return lax.ppermute(value, "dp", [(i, i ^ (1 << bit)) for i in range(count)])


def add(left, right):
    return (left.astype(f32) + right.astype(f32)).astype(left.dtype)


def shards(
    count,
    hidden_in,
    norm1_gain,
    w_query,
    w_key,
    w_value,
    w_output,
    bias_table,
    bucket_ids,
    norm2_gain,
    router,
    w_in,
    w_out,
    expert_ids,
    slot_ids,
    out_grad,
):
    tokens, width = hidden_in.shape
    buckets, heads = bias_table.shape
    experts = router.shape[1]
    capacity = max(2, 5 * tokens // (4 * experts))
    places = experts * capacity
    bits = (count - 1).bit_length()
    swap = [(0, 1), (1, 0)]
    mp = lax.axis_index("mp").astype(jnp.int32)
    dp = lax.axis_index("dp").astype(jnp.int32)
    side = (dp & 1)[None]
    where = jnp.stack([mp] + [(dp >> bit) & 1 for bit in range(bits)])

    def swapped(value):
        return lax.ppermute(value, "mp", swap)

    def to_experts(rows):
        block = rows.reshape(experts, capacity, -1)
        return lax.all_to_all(block, "dp", split_axis=0, concat_axis=0, tiled=True).reshape(
            places, -1
        )

    slot_row = (expert_ids[None, :], slot_ids[None, :])
    slot_column = (expert_ids * capacity + slot_ids)[:, None]

    w_near, _ = split(w_output, (dp & 1) == 0)
    w_near = swapped(w_near)
    c_here = to_experts(place(capacity, slot_row, out_grad, places))
    o, q, k, v, p, ids = attend(
        hidden_in, norm1_gain, w_query, w_key, w_value, bias_table.T, bucket_ids
    )
    o, w_near = lax.optimization_barrier((o, w_near))
    o_other = swapped(o)
    w_far = exchange(w_near, count, 0)
    hmid, x_send = middle(
        capacity, where, o, o_other, w_output, w_near, w_far, hidden_in, norm2_gain, slot_row, places
    )
    x_here = to_experts(x_send)

    dx, hid, dpre, deo, gate, dlog = expert(x_here, c_here, w_in[0], w_out[0], router.T, dp[None])
    dx_home = to_experts(dx)
    eo = (gate * dot(hid, w_out[0])).astype(bf16)
    eo_mine = jnp.where(mp == 0, eo[:, : width // 2], eo[:, width // 2 :])
    eo_other = swapped(jnp.where(mp == 0, eo[:, width // 2 :], eo[:, : width // 2]))
    grad_w_out = contract_rows(hid, deo)[None]
    grad_w_in = contract_rows(x_here, dpre)[None]
    grad_router = contract_rows(dlog, x_here.astype(f32), lax.Precision.HIGHEST)
    eo = add(eo_mine, eo_other)
    dx_home, grad_w_out, grad_w_in, grad_router = lax.optimization_barrier(
        (dx_home, grad_w_out, grad_w_in, grad_router)
    )

    first = 3 * tokens // 4
    low, high = pick(slot_column, dx_home, first, tokens - first)
    low, high, eo = lax.optimization_barrier((low, high, eo))
    low_other = swapped(low)
    high_other = swapped(high)
    eo_home = to_experts(eo)
    before = middle_back(0, low, low_other, hmid, out_grad, norm2_gain, w_output)
    dh, da, do, grad_norm2 = middle_back(
        first, high, high_other, hmid, out_grad, norm2_gain, w_output, before
    )
    dn1, keep, send = attend_back(
        side, do, q, k, v, p, w_query, w_key, w_value, o, da, hidden_in, norm1_gain, ids,
        grad_router, grad_norm2, buckets,
    )
    dn1, keep, send, eo_home = lax.optimization_barrier((dn1, keep, send, eo_home))
    dn1_other = swapped(dn1)

    local = q.shape[1]
    order_a = tuple(range(1, bits))
    order_b = (2, 1) + tuple(range(3, bits))
    got = exchange(send, count, 0)
    a, b = (keep[:local], got[:local]), (keep[local:], got[local:])
    for stage, (bit_a, bit_b) in enumerate(zip(order_a[:-1], order_b[:-1])):
        keep_a, send_a = split_sum(a, where[bit_a + 1] == 0)
        keep_b, send_b = split_sum(b, where[bit_b + 1] == 0)
        got_a = exchange(send_a, count, bit_a)
        got_b = exchange(send_b, count, bit_b)
        if stage == 0:
            (picked,) = pick(slot_column, eo_home, tokens)
            got_a, got_b, picked = lax.optimization_barrier((got_a, got_b, picked))
        a, b = (keep_a, got_a), (keep_b, got_b)
    a, b = add(*a), add(*b)
    got_a = exchange(a, count, order_a[-1])
    got_b = exchange(b, count, order_b[-1])
    grad_hidden = input_back(dn1, dn1_other, hidden_in, dh, norm1_gain)
    got_a, got_b, grad_hidden = lax.optimization_barrier((got_a, got_b, grad_hidden))
    picked_other = swapped(picked)
    a, b = add(a, got_a), add(b, got_b)
    for bit_a, bit_b in zip(order_a[-2::-1], order_b[-2::-1]):
        got_a = exchange(a, count, bit_a)
        got_b = exchange(b, count, bit_b)
        a = pair_up(a, got_a, where[bit_a + 1] == 0)
        b = pair_up(b, got_b, where[bit_b + 1] == 0)
        if bit_b == 1:
            small = b[local // 2 :]
            b = b[: local // 2]
            small_other = swapped(small)
    hidden_out = finish(where, picked, picked_other, hmid)
    a, b, small_other, hidden_out = lax.optimization_barrier((a, b, small_other, hidden_out))
    grad_q, grad_k, grad_v, grad_w_output, grad_router, grad_table, grad_norm1, grad_norm2 = unpack(
        where, a, exchange(a, count, 0), b, exchange(b, count, 0), small, small_other,
        experts, buckets, heads,
    )
    return (
        hidden_out,
        grad_hidden,
        grad_norm1,
        grad_q,
        grad_k,
        grad_v,
        grad_w_output,
        grad_table.T,
        grad_norm2,
        grad_router.T,
        grad_w_in,
        grad_w_out,
    )


def solution(mesh):
    return jax.shard_map(
        functools.partial(shards, mesh.shape["dp"]),
        mesh=mesh,
        in_specs=(
            P("dp", None),
            P(),
            P(None, "mp"),
            P(None, "mp"),
            P(None, "mp"),
            P("mp", None),
            P(None, "mp"),
            P(),
            P(),
            P(),
            P("dp", None, "mp"),
            P("dp", "mp", None),
            P("dp"),
            P("dp"),
            P("dp", None),
        ),
        out_specs=(
            P("dp", None),
            P("dp", None),
            P(),
            P(None, "mp"),
            P(None, "mp"),
            P(None, "mp"),
            P("mp", None),
            P(None, "mp"),
            P(),
            P(),
            P("dp", None, "mp"),
            P("dp", "mp", None),
        ),
        check_vma=False,
    )
```
